512 devices in a mesh: grid: 64 (over z_hi, y, core), comp: 8 (over x, z_lo).
Axes of the slice: x: 4, y: 8, z: 8 (z_hi: 4, z_lo: 2; z = z_hi * 2 + z_lo), core: 2. Of those that a mesh axis runs over, the one named last changes fastest.
Arguments:
- fields_runs: bfloat16 [1024, 131072], P('comp', 'grid'), may hold values from -16 to 16
- eof_basis: bfloat16 [131072, 512], P('grid', 'comp'), may hold values from -6 to 6
- weights_inv: float32 [1024, 1024], P(None, 'grid'), may hold values from -1 to 1
- design: float32 [8, 1024], replicated, may hold values from 0 to 1
- new_settings: float32 [8, 2048], replicated, may hold values from 0 to 1
- lscale: float32 [8, 512], P(None, 'comp'), may hold values from 0.5 to 4
- variance: float32 [512], P('comp'), may hold values from 0.5 to 2
Outputs:
- imitated: bfloat16 [2048, 131072], P('comp', 'grid')
The draws below stay inside these ranges and needn't reach their ends.
All inputs are finite; a program needn't handle non-finite values.
Results may differ from the reference program's by a relative error of at most 0.0049.
Values may be sent and summed in bfloat16 or wider, within the bound.
No kernel may reach another device: no remote copies, remote signals or barrier semaphores. Data moves between devices by JAX's collectives and lax.ppermute only.
A program may use at most 64 MiB of HBM per device.

```python
import math
import jax
import jax.numpy as jnp
from jax import lax

COMPS = 512
PARAMS = 8
CELLS = 131072
RUNS = 1024
SETTINGS = 2048


def draw_weights_inv(key, part):
    key = jax.random.fold_in(key, 11)
    first, second = jax.random.split(key, 2)
    diag = jax.random.uniform(first, (RUNS,), jnp.float32, 0.5, 1.5)
    offdiag = jnp.clip(jax.random.normal(second, (RUNS, RUNS), jnp.float32), -4.0, 4.0) * 0.3
    ident = (jnp.arange(RUNS)[:, None] == jnp.arange(RUNS)[None, :]).astype(jnp.float32)
    return (ident * diag[None, :] + offdiag / math.sqrt(RUNS)) / math.sqrt(RUNS)


def strengthened(array, own_key, source, target, shards_of, factor):
    owner, partner = [(jnp.arange(array.shape[dim]) // (array.shape[dim] // shards_of)).reshape([-1 if axis == dim else 1 for axis in range(array.ndim)]) for dim in (source, target)]
    chosen = jax.random.permutation(own_key, shards_of)[partner]
    strong = (owner == chosen) | (owner == (partner + shards_of // 2) % shards_of)
    return jnp.where(strong, factor * array, array)


def level_of(key, dims, shards, least, largest):
    gain = 1.0
    for position, shards_of in shards:
        steps = jax.random.uniform(jax.random.fold_in(jax.random.fold_in(key, 6), position), (shards_of,), jnp.float32, least / len(shards), largest / len(shards))
        gain = gain * jnp.repeat(jnp.exp(steps), dims[position] // shards_of).reshape((-1,) + (1,) * (len(dims) - 1 - position))
    return gain


def bell_draw(own_key, extent, deviation, reach, shards=(), kind=jnp.bfloat16):
    array = deviation * jax.random.normal(own_key, extent, jnp.float32)
    if shards:
        array = array * level_of(own_key, extent, shards, -0.22, 0.18)
    return jnp.clip(array, -reach, reach).astype(kind)


def noise_with(rng, shape, deviation, bound, cuts, heavy, dtype=jnp.bfloat16):
    result = deviation * jax.random.normal(rng, shape, jnp.float32)
    if cuts:
        result = result * level_of(rng, shape, cuts, -0.22, 0.18)
    return jnp.clip(strengthened(result, jax.random.fold_in(rng, 3), *heavy), -bound, bound).astype(dtype)


def setup_inputs(seed: int = 0) -> dict:
    keys = jax.random.split(jax.random.key(seed), 8)
    return {
        "fields_runs": noise_with(keys[0], (RUNS, CELLS), 1.0, 16.0, ((0, 8), (1, 64)), (1, 0, 64, 4.0)),
        "eof_basis": bell_draw(keys[1], (CELLS, COMPS), 1.0, 6.0, ((0, 64), (1, 8))),
        "weights_inv": draw_weights_inv(jax.random.fold_in(keys[7], 71), 0),
        "design": jnp.clip(jax.random.uniform(keys[3], (PARAMS, RUNS), jnp.float32, 0.0, 1.0), 0.0, 1.0),
        "new_settings": jnp.clip(jax.random.uniform(keys[4], (PARAMS, SETTINGS), jnp.float32, 0.0, 1.0), 0.0, 1.0),
        "lscale": jnp.clip(jnp.exp(math.log(4.0) - 2.0794415 * jax.random.uniform(keys[5], (PARAMS, COMPS), jnp.float32) ** level_of(keys[5], (PARAMS, COMPS), ((1, 8),), -0.2, 0.2)), 0.5, 4.0),
        "variance": jnp.clip(jnp.exp(math.log(2.0) - 1.3862944 * jax.random.uniform(keys[6], (COMPS,), jnp.float32) ** level_of(keys[6], (COMPS,), ((0, 8),), -0.2, 0.2)), 0.5, 2.0),
    }


SQRT_THREE = 1.7320508075688772

def matern_block(lscale, variance, alpha, settings, design):
    kblock = lscale.shape[1]
    sq = jnp.zeros((kblock, settings.shape[1], design.shape[1]), jnp.float32)
    for param in range(lscale.shape[0]):
        diff = settings[param][:, None] - design[param][None, :]
        sq = sq + (diff[None, :, :] / lscale[param][:, None, None]) ** 2
    radius = jnp.sqrt(sq)
    cross = variance[:, None, None] * (1.0 + SQRT_THREE * radius) * jnp.exp(-SQRT_THREE * radius)
    return jnp.einsum('kni,ik->nk', cross, alpha, precision=lax.Precision.HIGHEST)

def reference(fields_runs, eof_basis, weights_inv, design, new_settings, lscale, variance):
    coef = jnp.dot(fields_runs, eof_basis, preferred_element_type=jnp.float32) * (1.0 / math.sqrt(CELLS))
    alpha = jnp.dot(weights_inv, coef, precision=lax.Precision.HIGHEST)
    blocks = COMPS // 8
    scale_blocks = lscale.reshape(PARAMS, blocks, 8).transpose(1, 0, 2)
    var_blocks = variance.reshape(blocks, 8)
    alpha_blocks = alpha.reshape(RUNS, blocks, 8).transpose(1, 0, 2)

    def one_block(items):
        return matern_block(items[0], items[1], items[2], new_settings, design)
    pred = lax.map(one_block, (scale_blocks, var_blocks, alpha_blocks))
    pred = pred.transpose(1, 0, 2).reshape(SETTINGS, COMPS).astype(jnp.bfloat16)
    imitated = jnp.dot(pred, eof_basis.T, preferred_element_type=jnp.float32) * (1.0 / math.sqrt(COMPS))
    return imitated.astype(jnp.bfloat16)
```

```python
import math

import jax
import jax.numpy as jnp
from jax import lax
from jax.experimental import pallas as pl
from jax.experimental.pallas import tpu as pltpu
from jax.sharding import Mesh, PartitionSpec as P

GRID = ("zh", "y", "core")
COMP = ("x", "zl")
LOG2E = 1.4426950408889634
LN2 = 0.6931471805599453
F32 = jnp.float32
BF16 = jnp.bfloat16
HIGHEST = lax.Precision.HIGHEST
VMEM = pl.BlockSpec(memory_space=pltpu.VMEM)
SMEM = pl.BlockSpec(memory_space=pltpu.SMEM)


def params(mib):
    return pltpu.CompilerParams(vmem_limit_bytes=mib << 20)


def project_kernel(scale, own_ref, other_ref, basis_ref, out_ref):
    for half, runs_ref in enumerate((own_ref, other_ref)):
        part = lax.dot_general(
            basis_ref[...], runs_ref[...], (((1,), (1,)), ((), ())), preferred_element_type=F32
        )
        part = part * scale
        for block in range(4):
            out_ref[pl.ds(4 * half + block, 64, stride=8), :] = part[64 * block : 64 * block + 64]


def project(own, other, basis, scale):
    def body(*refs):
        project_kernel(scale, *refs)

    return pl.pallas_call(
        body,
        out_shape=jax.ShapeDtypeStruct((512, 128), F32),
        in_specs=[VMEM] * 3,
        out_specs=VMEM,
        compiler_params=params(16),
        cost_estimate=pl.CostEstimate(flops=1 << 28, bytes_accessed=1 << 21, transcendentals=0),
    )(own, other, basis)


def weights_kernel(place_ref, parts_ref, winv_ref, out_ref):
    coef = jnp.sum(parts_ref[...], axis=0)
    place = place_ref[0]
    own = jnp.dot(
        coef, winv_ref[pl.ds(pl.multiple_of(place * 128, 128), 128), :],
        precision=HIGHEST, preferred_element_type=F32,
    )
    other = jnp.dot(
        coef, winv_ref[pl.ds(pl.multiple_of((1 - place) * 128, 128), 128), :],
        precision=HIGHEST, preferred_element_type=F32,
    )
    row = lax.broadcasted_iota(jnp.int32, own.shape, 0)
    both = jnp.where(row < 4, own, other)
    for peer in range(4):
        out_ref[peer] = both


def weights(place, parts, winv):
    return pl.pallas_call(
        weights_kernel,
        out_shape=jax.ShapeDtypeStruct((4, 8, 1024), F32),
        in_specs=[SMEM, VMEM, VMEM],
        out_specs=VMEM,
        compiler_params=params(16),
        cost_estimate=pl.CostEstimate(flops=1 << 23, bytes_accessed=1 << 20, transcendentals=0),
    )(place, parts, winv)


def cross_kernel(var_ref, runs_ref, new_ref, out_ref):
    var = var_ref[pl.program_id(0)]
    for chunk in range(4):
        rows = slice(64 * chunk, 64 * chunk + 64)
        sq = jnp.dot(runs_ref[0, rows], new_ref[0], precision=HIGHEST, preferred_element_type=F32)
        sq = jnp.maximum(sq, 1e-30)
        dist = sq * lax.rsqrt(sq)
        out_ref[0, rows] = (var + (var * LN2) * dist) * jnp.exp2(-dist)


def cross_all(var, runs_feat, new_feat):
    return pl.pallas_call(
        cross_kernel,
        grid=(4, 4),
        out_shape=jax.ShapeDtypeStruct((4, 1024, 512), F32),
        in_specs=[
            SMEM,
            pl.BlockSpec((1, 256, 16), lambda b, i: (b, i, 0)),
            pl.BlockSpec((1, 16, 512), lambda b, i: (b, 0, 0)),
        ],
        out_specs=pl.BlockSpec((1, 256, 512), lambda b, i: (b, i, 0)),
        compiler_params=params(16),
        cost_estimate=pl.CostEstimate(
            flops=1 << 28, bytes_accessed=1 << 23, transcendentals=1 << 22
        ),
    )(var, runs_feat, new_feat)


def predict_kernel(cross_ref, pieces_ref, out_ref, spread_ref, pred_ref):
    block = pl.program_id(0)

    @pl.when(block == 0)
    def _():
        both = jnp.sum(pieces_ref[...], axis=0)
        first = both.astype(BF16)
        rest = both - first.astype(F32)
        second = rest.astype(BF16)
        third = (rest - second.astype(F32)).astype(BF16)
        lhs = jnp.concatenate([first.astype(F32), second.astype(F32), third.astype(F32)], axis=0)
        row = lax.broadcasted_iota(jnp.int32, (24, 512), 0)
        col = lax.broadcasted_iota(jnp.int32, (24, 512), 1)
        pick = (row % 4 == col // 128).astype(BF16)
        spread_ref[...] = jnp.dot(lhs.T.astype(BF16), pick, preferred_element_type=F32)

    def step(index, acc):
        base = pl.multiple_of(index * 64, 64)
        lanes = pl.ds(pl.multiple_of(block * 128, 128), 128)
        weight = spread_ref[pl.ds(base, 64), lanes]
        values = cross_ref[0, pl.ds(base, 64), :]
        sums = []
        for tile in range(4):
            prod = values[:, 128 * tile : 128 * tile + 128] * weight
            sums.append(jnp.sum(prod.reshape(8, 8, 128), axis=0))
        return tuple(a + s for a, s in zip(acc, sums))

    zero = jnp.zeros((8, 128), F32)
    acc = lax.fori_loop(0, 16, step, (zero,) * 4, unroll=2)
    for tile in range(4):
        where = (tile // 2) * 8 + 2 * block + tile % 2
        pred_ref[pl.ds(where, 1), :] = jnp.sum(acc[tile], axis=0, keepdims=True)

    @pl.when(block == 3)
    def _():
        tile = pred_ref[...].astype(BF16).reshape(1, 2, 8, 128)
        out_ref[...] = jnp.broadcast_to(tile, (64, 2, 8, 128))


def predict(cross, pieces):
    return pl.pallas_call(
        predict_kernel,
        grid=(4,),
        out_shape=jax.ShapeDtypeStruct((64, 2, 8, 128), BF16),
        in_specs=[
            pl.BlockSpec((1, 1024, 512), lambda b: (b, 0, 0)),
            pl.BlockSpec((4, 8, 1024), lambda b: (0, 0, 0)),
        ],
        out_specs=pl.BlockSpec((64, 2, 8, 128), lambda b: (0, 0, 0, 0)),
        scratch_shapes=[pltpu.VMEM((1024, 512), F32), pltpu.VMEM((16, 128), F32)],
        compiler_params=params(16),
        cost_estimate=pl.CostEstimate(flops=1 << 22, bytes_accessed=1 << 23, transcendentals=0),
    )(cross, pieces)


def rebuild_kernel(scale, place_ref, pred_ref, own_ref, other_ref, out_ref, wide_ref, lhs_ref):
    @pl.when(pl.program_id(0) == 0)
    def _():
        wide_ref[...] = pred_ref[...].astype(F32).reshape(1024, 128)
        place = place_ref[0]
        for side, which in enumerate((place, 1 - place)):
            rows = []
            for block in range(4):
                halves = [
                    wide_ref[pl.ds(8 * which + 2 * block + half, 64, stride=16), :]
                    for half in range(2)
                ]
                rows.append(jnp.concatenate(halves, axis=1))
            table = jnp.concatenate(rows, axis=0)
            lhs_ref[:, 256 * side : 256 * side + 256] = table.T.astype(BF16)

    total = jnp.dot(lhs_ref[:, :256], own_ref[...], preferred_element_type=F32)
    total = total + jnp.dot(lhs_ref[:, 256:], other_ref[...], preferred_element_type=F32)
    out_ref[...] = (total * scale).astype(BF16)


def rebuild(place, pred, own, other, scale):
    def body(*refs):
        rebuild_kernel(scale, *refs)

    width = 512
    return pl.pallas_call(
        body,
        grid=(2048 // width,),
        out_shape=jax.ShapeDtypeStruct((256, 2048), BF16),
        in_specs=[
            SMEM,
            pl.BlockSpec((64, 2, 8, 128), lambda i: (0, 0, 0, 0)),
            pl.BlockSpec((256, width), lambda i: (0, i)),
            pl.BlockSpec((256, width), lambda i: (0, i)),
        ],
        out_specs=pl.BlockSpec((256, width), lambda i: (0, i)),
        scratch_shapes=[pltpu.VMEM((1024, 128), F32), pltpu.VMEM((256, 512), BF16)],
        compiler_params=params(16),
        cost_estimate=pl.CostEstimate(flops=1 << 29, bytes_accessed=3 << 20, transcendentals=0),
    )(place, pred, own, other)


def kernel_params(lscale, variance, place, x):
    mine = jnp.concatenate([lscale, variance[None, :]], axis=0)
    mine = lax.dynamic_slice_in_dim(mine, place, 1, axis=1)
    mine = jnp.broadcast_to(jnp.pad(mine, ((0, 7), (0, 0))), (16, 128))
    by_shift = [mine]
    for shift in range(1, 4):
        by_shift.append(lax.ppermute(mine, "x", [(i, (i + shift) % 4) for i in range(4)]))
    stacked = jnp.stack([v[:9, 0] for v in by_shift])
    pick = (x - jnp.arange(4)) % 4
    chosen = jnp.sum(
        jnp.where(pick[:, None, None] == jnp.arange(4)[None, :, None], stacked[None], 0.0), axis=1
    )
    return chosen[:, :8], chosen[:, 8]


def features(lscale, design, new_settings, x):
    weight = (3.0 * LOG2E * LOG2E) / (lscale * lscale)
    new = lax.dynamic_slice_in_dim(new_settings, x * 512, 512, axis=1) - 0.5
    runs = design.T - 0.5
    ones_new = jnp.ones((4, 1, 512), F32)
    new_feat = jnp.concatenate(
        [
            -2.0 * weight[:, :, None] * new[None],
            ones_new,
            jnp.sum(weight[:, :, None] * (new * new)[None], axis=1, keepdims=True),
            jnp.zeros((4, 6, 512), F32),
        ],
        axis=1,
    )
    runs_feat = jnp.concatenate(
        [
            jnp.broadcast_to(runs[None], (4, 1024, 8)),
            jnp.sum((runs * runs)[None] * weight[:, None, :], axis=2, keepdims=True),
            jnp.ones((4, 1024, 1), F32),
            jnp.zeros((4, 1024, 6), F32),
        ],
        axis=2,
    )
    return runs_feat, new_feat


def on_device(fields_runs, eof_basis, weights_inv, design, new_settings, lscale, variance):
    x = lax.axis_index("x")
    place = lax.axis_index(GRID)
    zl = lax.axis_index("zl").reshape(1)
    swap = [(0, 1), (1, 0)]

    fields_other = lax.ppermute(fields_runs, "zl", swap)
    basis = lax.all_to_all(
        jnp.broadcast_to(eof_basis.T[None], (4, 64, 2048)), "x", 0, 0, tiled=True
    ).reshape(256, 2048)
    winv = lax.ppermute(
        weights_inv.T, ("zh", "x"), [(a * 4 + b, b * 4 + a) for a in range(4) for b in range(4)]
    )
    winv = lax.all_gather(winv, ("y", "core"), axis=0, tiled=True)

    scales, var = kernel_params(lscale, variance, place, x)
    runs_feat, new_feat = features(scales, design, new_settings, x)
    cross = cross_all(var, runs_feat, new_feat)

    partial = project(fields_runs, fields_other, basis, 1.0 / math.sqrt(131072))
    parts = lax.all_to_all(partial.reshape(64, 8, 128), GRID, 0, 0, tiled=True)
    basis_other = lax.ppermute(basis, "zl", swap)

    pieces = lax.all_to_all(weights(zl, parts, winv), "x", 0, 0, tiled=True)
    pred = predict(cross, pieces)
    pred = lax.all_to_all(pred.reshape(128, 8, 128), GRID + ("zl",), 0, 0, tiled=True)
    return rebuild(zl, pred.reshape(64, 2, 8, 128), basis, basis_other, 1.0 / math.sqrt(512))


def solution(mesh):
    fine = Mesh(mesh.devices.reshape(4, 8, 2, 4, 2), GRID + COMP)
    placed = (
        P(COMP, GRID),
        P(GRID, COMP),
        P(None, GRID),
        P(),
        P(),
        P(None, COMP),
        P(COMP),
    )
    return jax.shard_map(
        on_device, mesh=fine, in_specs=placed, out_specs=P(COMP, GRID), check_vma=False
    )
```

```python
import math

import jax
import jax.numpy as jnp
from jax import lax
from jax.experimental import pallas as pl
from jax.experimental.pallas import tpu as pltpu
from jax.sharding import Mesh, PartitionSpec as P

GRID = ("zh", "y", "core")
COMP = ("x", "zl")
LOG2E = 1.4426950408889634
LN2 = 0.6931471805599453
F32 = jnp.float32
BF16 = jnp.bfloat16
HIGHEST = lax.Precision.HIGHEST
VMEM = pl.BlockSpec(memory_space=pltpu.VMEM)
SMEM = pl.BlockSpec(memory_space=pltpu.SMEM)
CELLS = 2048
WIDE = CELLS + 128


def params(mib):
    return pltpu.CompilerParams(vmem_limit_bytes=mib << 20)


def split3(value):
    first = value.astype(BF16)
    rest = value - first.astype(F32)
    second = rest.astype(BF16)
    third = (rest - second.astype(F32)).astype(BF16)
    return first, second, third


def pack_kernel(basis_ref, lscale_ref, variance_ref, out_ref):
    row = lax.broadcasted_iota(jnp.int32, (8, 64), 0)
    tail = jnp.where(row == 0, jnp.broadcast_to(variance_ref[...], (8, 64)), 0.0)
    value = jnp.concatenate([lscale_ref[...], tail], axis=0)
    pieces = jnp.concatenate([part.astype(F32) for part in split3(value)], axis=0)
    pieces = jnp.concatenate([pieces, jnp.zeros((80, 64), F32)], axis=0)
    side = jnp.concatenate([pieces, jnp.zeros((128, 64), F32)], axis=1).T[:64].astype(BF16)
    basis = basis_ref[...]
    for peer in range(4):
        out_ref[peer, :, :CELLS] = basis
        out_ref[peer, :, CELLS:] = side


def pack(basis, lscale, variance):
    return pl.pallas_call(
        pack_kernel,
        out_shape=jax.ShapeDtypeStruct((4, 64, WIDE), BF16),
        in_specs=[VMEM] * 3,
        out_specs=VMEM,
        compiler_params=params(16),
        cost_estimate=pl.CostEstimate(flops=0, bytes_accessed=5 << 18, transcendentals=0),
    )(basis, lscale, variance)


def project_kernel(scale, own_ref, other_ref, basis_ref, out_ref):
    for half, runs_ref in enumerate((own_ref, other_ref)):
        part = lax.dot_general(
            basis_ref[:, :CELLS], runs_ref[...], (((1,), (1,)), ((), ())), preferred_element_type=F32
        )
        part = part * scale
        for block in range(4):
            out_ref[pl.ds(4 * half + block, 64, stride=8), :] = part[64 * block : 64 * block + 64]


def project(own, other, basis, scale):
    def body(*refs):
        project_kernel(scale, *refs)

    return pl.pallas_call(
        body,
        out_shape=jax.ShapeDtypeStruct((512, 128), F32),
        in_specs=[VMEM] * 3,
        out_specs=VMEM,
        compiler_params=params(16),
        cost_estimate=pl.CostEstimate(flops=1 << 28, bytes_accessed=1 << 21, transcendentals=0),
    )(own, other, basis)


def weights_kernel(place_ref, parts_ref, winv_ref, after_ref, out_ref):
    coef = jnp.sum(parts_ref[...], axis=0)
    place = place_ref[0]
    own = jnp.dot(
        coef, winv_ref[pl.ds(pl.multiple_of(place * 128, 128), 128), :],
        precision=HIGHEST, preferred_element_type=F32,
    )
    other = jnp.dot(
        coef, winv_ref[pl.ds(pl.multiple_of((1 - place) * 128, 128), 128), :],
        precision=HIGHEST, preferred_element_type=F32,
    )
    row = lax.broadcasted_iota(jnp.int32, own.shape, 0)
    both = jnp.where(row < 4, own, other)
    for peer in range(4):
        out_ref[peer] = both


def weights(place, parts, winv, after):
    return pl.pallas_call(
        weights_kernel,
        out_shape=jax.ShapeDtypeStruct((4, 8, 1024), F32),
        in_specs=[SMEM, VMEM, VMEM, pl.BlockSpec(memory_space=pl.ANY)],
        out_specs=VMEM,
        compiler_params=params(16),
        cost_estimate=pl.CostEstimate(flops=1 << 23, bytes_accessed=1 << 20, transcendentals=0),
    )(place, parts, winv, after)


def cross_kernel(where_ref, side_ref, design_ref, new_ref, out_ref, aux_ref, side_wide, runs_feat):
    block = pl.program_id(0)

    @pl.when(block == 0)
    def _():
        side_wide[...] = side_ref[...].astype(F32)
        runs = design_ref[...] - 0.5
        first, second, third = split3(jnp.concatenate([runs, runs * runs], axis=0))
        row = lax.broadcasted_iota(jnp.int32, (32, 1024), 0)
        ones = jnp.where(row < 3, 1.0, 0.0)
        parts = [first, first, first, second, second, third]
        table = jnp.concatenate([p.astype(F32) for p in parts] + [ones], axis=0)
        runs_feat[...] = table.T.astype(BF16)

    mine = side_wide[pl.ds(64 * block + where_ref[1], 1), :]
    column = jnp.broadcast_to(mine, (128, 128)).T
    value = (column[0:16] + column[16:32]) + column[32:48]
    aux_ref[pl.ds(block, 1), :] = value[8:9] * LN2
    lscale = value[:8]
    weight = (3.0 * LOG2E * LOG2E) / (lscale * lscale)
    weight = jnp.concatenate([weight] * 4, axis=1)
    new = new_ref[:, pl.ds(pl.multiple_of(where_ref[0] * 512, 512), 512)] - 0.5
    scaled = weight * new
    first, second, third = split3(jnp.concatenate([-2.0 * scaled, weight], axis=0))
    square = jnp.broadcast_to(jnp.sum(scaled * new, axis=0, keepdims=True), (32, 512))
    row = lax.broadcasted_iota(jnp.int32, (32, 512), 0)
    lead, mid, low = [p.astype(F32) for p in split3(square)]
    tail = jnp.where(row == 0, lead, jnp.where(row == 1, mid, jnp.where(row == 2, low, 0.0)))
    rhs = jnp.concatenate([first, second, third, first, second, first, tail.astype(BF16)], axis=0)
    for chunk in range(16):
        rows = slice(64 * chunk, 64 * chunk + 64)
        sq = jnp.dot(runs_feat[rows], rhs, preferred_element_type=F32)
        sq = jnp.maximum(sq, 1e-30)
        dist = sq * lax.rsqrt(sq)
        out_ref[0, rows] = (LOG2E + dist) * jnp.exp2(-dist)


def cross_all(where, basis, design, new_settings):
    return pl.pallas_call(
        cross_kernel,
        grid=(4,),
        out_shape=(
            jax.ShapeDtypeStruct((4, 1024, 512), F32),
            jax.ShapeDtypeStruct((8, 128), F32),
        ),
        in_specs=[
            SMEM,
            pl.BlockSpec((256, 128), lambda b: (0, CELLS // 128)),
            pl.BlockSpec((8, 1024), lambda b: (0, 0)),
            pl.BlockSpec((8, 2048), lambda b: (0, 0)),
        ],
        out_specs=(
            pl.BlockSpec((1, 1024, 512), lambda b: (b, 0, 0)),
            pl.BlockSpec((8, 128), lambda b: (0, 0)),
        ),
        scratch_shapes=[pltpu.VMEM((256, 128), F32), pltpu.VMEM((1024, 128), BF16)],
        compiler_params=params(16),
        cost_estimate=pl.CostEstimate(
            flops=1 << 28, bytes_accessed=1 << 23, transcendentals=1 << 22
        ),
    )(where, basis, design, new_settings)


def predict_kernel(cross_ref, pieces_ref, aux_ref, out_ref, spread_ref, pred_ref):
    block = pl.program_id(0)

    @pl.when(block == 0)
    def _():
        both = jnp.sum(pieces_ref[...], axis=0)
        lhs = jnp.concatenate([p.astype(F32) for p in split3(both)], axis=0)
        row = lax.broadcasted_iota(jnp.int32, (24, 512), 0)
        col = lax.broadcasted_iota(jnp.int32, (24, 512), 1)
        pick = (row % 4 == col // 128).astype(BF16)
        spread_ref[...] = jnp.dot(lhs.T.astype(BF16), pick, preferred_element_type=F32)

    def step(index, acc):
        base = pl.multiple_of(index * 64, 64)
        lanes = pl.ds(pl.multiple_of(block * 128, 128), 128)
        weight = spread_ref[pl.ds(base, 64), lanes]
        values = cross_ref[0, pl.ds(base, 64), :]
        sums = []
        for tile in range(4):
            prod = values[:, 128 * tile : 128 * tile + 128] * weight
            sums.append(jnp.sum(prod.reshape(8, 8, 128), axis=0))
        return tuple(a + s for a, s in zip(acc, sums))

    zero = jnp.zeros((8, 128), F32)
    acc = lax.fori_loop(0, 16, step, (zero,) * 4, unroll=2)
    for tile in range(4):
        where = (tile // 2) * 8 + 2 * block + tile % 2
        total = jnp.sum(acc[tile], axis=0, keepdims=True)
        pred_ref[pl.ds(where, 1), :] = total * aux_ref[pl.ds(block, 1), :]

    @pl.when(block == 3)
    def _():
        tile = pred_ref[...].astype(BF16).reshape(1, 2, 8, 128)
        out_ref[...] = jnp.broadcast_to(tile, (64, 2, 8, 128))


def predict(cross, pieces, aux):
    return pl.pallas_call(
        predict_kernel,
        grid=(4,),
        out_shape=jax.ShapeDtypeStruct((64, 2, 8, 128), BF16),
        in_specs=[
            pl.BlockSpec((1, 1024, 512), lambda b: (b, 0, 0)),
            pl.BlockSpec((4, 8, 1024), lambda b: (0, 0, 0)),
            pl.BlockSpec((8, 128), lambda b: (0, 0)),
        ],
        out_specs=pl.BlockSpec((64, 2, 8, 128), lambda b: (0, 0, 0, 0)),
        scratch_shapes=[pltpu.VMEM((1024, 512), F32), pltpu.VMEM((16, 128), F32)],
        compiler_params=params(16),
        cost_estimate=pl.CostEstimate(flops=1 << 22, bytes_accessed=1 << 23, transcendentals=0),
    )(cross, pieces, aux)


def rebuild_kernel(scale, place_ref, pred_ref, own_ref, other_ref, out_ref, wide_ref, lhs_ref):
    @pl.when(pl.program_id(0) == 0)
    def _():
        wide_ref[...] = pred_ref[...].astype(F32).reshape(1024, 128)
        place = place_ref[0]
        for side, which in enumerate((place, 1 - place)):
            rows = []
            for block in range(4):
                halves = [
                    wide_ref[pl.ds(8 * which + 2 * block + half, 64, stride=16), :]
                    for half in range(2)
                ]
                rows.append(jnp.concatenate(halves, axis=1))
            table = jnp.concatenate(rows, axis=0)
            lhs_ref[:, 256 * side : 256 * side + 256] = table.T.astype(BF16)

    total = jnp.dot(lhs_ref[:, :256], own_ref[...], preferred_element_type=F32)
    total = total + jnp.dot(lhs_ref[:, 256:], other_ref[...], preferred_element_type=F32)
    out_ref[...] = (total * scale).astype(BF16)


def rebuild(place, pred, own, other, scale):
    def body(*refs):
        rebuild_kernel(scale, *refs)

    width = 512
    return pl.pallas_call(
        body,
        grid=(2048 // width,),
        out_shape=jax.ShapeDtypeStruct((256, 2048), BF16),
        in_specs=[
            SMEM,
            pl.BlockSpec((64, 2, 8, 128), lambda i: (0, 0, 0, 0)),
            pl.BlockSpec((256, width), lambda i: (0, i)),
            pl.BlockSpec((256, width), lambda i: (0, i)),
        ],
        out_specs=pl.BlockSpec((256, width), lambda i: (0, i)),
        scratch_shapes=[pltpu.VMEM((1024, 128), F32), pltpu.VMEM((256, 512), BF16)],
        compiler_params=params(16),
        cost_estimate=pl.CostEstimate(flops=1 << 29, bytes_accessed=3 << 20, transcendentals=0),
    )(place, pred, own, other)


def on_device(fields_runs, eof_basis, weights_inv, design, new_settings, lscale, variance):
    x = lax.axis_index("x")
    zl = lax.axis_index("zl").reshape(1)
    where = jnp.stack([x, lax.axis_index(GRID)])
    swap = [(0, 1), (1, 0)]
    own = eof_basis.T

    fields_other = lax.ppermute(fields_runs, "zl", swap)
    basis = lax.all_to_all(
        pack(own, lscale, variance.reshape(1, 64)), "x", 0, 0, tiled=True
    ).reshape(256, WIDE)
    winv = lax.ppermute(
        weights_inv.T, ("zh", "x"), [(a * 4 + b, b * 4 + a) for a in range(4) for b in range(4)]
    )
    winv = lax.all_gather(winv, "core", axis=0, tiled=True)
    winv = lax.all_gather(winv, "y", axis=0, tiled=True)

    partial = project(fields_runs, fields_other, basis, 1.0 / math.sqrt(131072))
    parts = lax.all_to_all(partial.reshape(64, 8, 128), GRID, 0, 0, tiled=True)

    cross, aux = cross_all(where, basis, design, new_settings)
    own, _ = lax.optimization_barrier((own, partial))
    basis_other = lax.all_gather(lax.ppermute(own, "zl", swap), "x", axis=0, tiled=True)

    pieces = lax.all_to_all(weights(zl, parts, winv, aux), "x", 0, 0, tiled=True)
    pred = predict(cross, pieces, aux)
    pred = lax.all_to_all(pred.reshape(128, 8, 128), GRID + ("zl",), 0, 0, tiled=True)
    return rebuild(zl, pred.reshape(64, 2, 8, 128), basis, basis_other, 1.0 / math.sqrt(512))


def solution(mesh):
    fine = Mesh(mesh.devices.reshape(4, 8, 2, 4, 2), GRID + COMP)
    placed = (
        P(COMP, GRID),
        P(GRID, COMP),
        P(None, GRID),
        P(),
        P(),
        P(None, COMP),
        P(COMP),
    )
    return jax.shard_map(
        on_device, mesh=fine, in_specs=placed, out_specs=P(COMP, GRID), check_vma=False
    )
```

```python
import math

import jax
import jax.numpy as jnp
from jax import lax
from jax.experimental import pallas as pl
from jax.experimental.pallas import tpu as pltpu
from jax.sharding import Mesh, PartitionSpec as P

GRID = ("zh", "y", "core")
COMP = ("x", "zl")
LOG2E = 1.4426950408889634
LN2 = 0.6931471805599453
F32 = jnp.float32
BF16 = jnp.bfloat16
HIGHEST = lax.Precision.HIGHEST
VMEM = pl.BlockSpec(memory_space=pltpu.VMEM)
SMEM = pl.BlockSpec(memory_space=pltpu.SMEM)
CELLS = 2048
WIDE = CELLS + 128


def params(mib):
    return pltpu.CompilerParams(vmem_limit_bytes=mib << 20)


def split3(value):
    first = value.astype(BF16)
    rest = value - first.astype(F32)
    second = rest.astype(BF16)
    third = (rest - second.astype(F32)).astype(BF16)
    return first, second, third


def pack_kernel(basis_ref, lscale_ref, variance_ref, out_ref):
    row = lax.broadcasted_iota(jnp.int32, (8, 64), 0)
    tail = jnp.where(row == 0, jnp.broadcast_to(variance_ref[...], (8, 64)), 0.0)
    value = jnp.concatenate([lscale_ref[...], tail], axis=0)
    pieces = jnp.concatenate([part.astype(F32) for part in split3(value)], axis=0)
    pieces = jnp.concatenate([pieces, jnp.zeros((80, 64), F32)], axis=0)
    side = jnp.concatenate([pieces, jnp.zeros((128, 64), F32)], axis=1).T[:64].astype(BF16)
    basis = basis_ref[...]
    for peer in range(4):
        out_ref[peer, :, :CELLS] = basis
        out_ref[peer, :, CELLS:] = side


def pack(basis, lscale, variance):
    return pl.pallas_call(
        pack_kernel,
        out_shape=jax.ShapeDtypeStruct((4, 64, WIDE), BF16),
        in_specs=[VMEM] * 3,
        out_specs=VMEM,
        compiler_params=params(16),
        cost_estimate=pl.CostEstimate(flops=0, bytes_accessed=5 << 18, transcendentals=0),
    )(basis, lscale, variance)


def project_kernel(scale, where_ref, own_ref, other_ref, basis_ref, pair_ref, out_ref, runs_ref, wide_ref):
    zl = where_ref[2]
    for half, fields_ref in ((zl, own_ref), (1 - zl, other_ref)):
        for y in range(4):
            for core in range(2):
                first = pl.multiple_of(128 * core + 64 * half + 16 * y, 16)
                from_row = 32 * y + 16 * core
                runs_ref[pl.ds(first, 16), :] = fields_ref[from_row : from_row + 16]
    part = lax.dot_general(
        basis_ref[:, :CELLS], runs_ref[...], (((1,), (1,)), ((), ())), preferred_element_type=F32
    )
    part = part * scale
    high = part.astype(BF16).astype(F32)
    lanes = pl.ds(pl.multiple_of(128 * where_ref[3], 128), 128)
    for half in range(2):
        for block in range(4):
            for core in range(2):
                first = 64 * block + 32 * core
                row = 16 * half + 4 * core + block
                piece = (slice(first, first + 32), slice(128 * half, 128 * half + 128))
                wide_ref[pl.ds(row, 32, stride=32), :] = high[piece]
                wide_ref[pl.ds(row + 8, 32, stride=32), :] = part[piece] - high[piece]
        mine = pair_ref[16 * half : 16 * half + 16, lanes]
        for chip in range(32):
            out_ref[2 * chip + half, 16:, :] = mine
    out_ref[:, :16, :] = wide_ref[...].astype(BF16).reshape(64, 16, 128)


def project(where, own, other, basis, pair, scale):
    def body(*refs):
        project_kernel(scale, *refs)

    return pl.pallas_call(
        body,
        out_shape=jax.ShapeDtypeStruct((64, 32, 128), BF16),
        in_specs=[SMEM] + [VMEM] * 4,
        out_specs=VMEM,
        scratch_shapes=[pltpu.VMEM((256, CELLS), BF16), pltpu.VMEM((1024, 128), F32)],
        compiler_params=params(16),
        cost_estimate=pl.CostEstimate(flops=1 << 28, bytes_accessed=1 << 21, transcendentals=0),
    )(where, own, other, basis, pair)


def weights_kernel(parts_ref, out_ref, winv_ref):
    for device in range(64):
        slot, y = 2 * (device // 16) + device % 2, device // 2 % 8
        winv_ref[16 * y : 16 * y + 16, 128 * slot : 128 * slot + 128] = parts_ref[device, 16:, :]
    both = jnp.sum(parts_ref[:, :16, :].astype(F32), axis=0)
    coef = both[:8] + both[8:]
    rows = jnp.concatenate(
        [p.astype(F32) for p in split3(coef)] + [jnp.zeros((8, 128), F32)], axis=0
    ).astype(BF16)
    full = jnp.dot(rows, winv_ref[...], preferred_element_type=F32)
    full = (full[16:24] + full[8:16]) + full[:8]
    for core in range(2):
        for block in range(4):
            for tile in range(8):
                piece = full[4 * core + block : 4 * core + block + 1, 128 * tile : 128 * tile + 128]
                for peer in range(4):
                    row = 8 * block + tile
                    out_ref[2 * peer + core, row : row + 1, :] = piece


def weights(parts):
    return pl.pallas_call(
        weights_kernel,
        out_shape=jax.ShapeDtypeStruct((8, 32, 128), F32),
        in_specs=[VMEM],
        out_specs=VMEM,
        scratch_shapes=[pltpu.VMEM((128, 1024), BF16)],
        compiler_params=params(16),
        cost_estimate=pl.CostEstimate(flops=1 << 23, bytes_accessed=1 << 20, transcendentals=0),
    )(parts)


def prepare_kernel(where_ref, side_ref, design_ref, new_ref, runs_ref, new_out_ref, aux_ref, wide_ref):
    wide_ref[...] = side_ref[...].astype(F32)
    runs = design_ref[...] - 0.5
    first, second, third = split3(jnp.concatenate([runs, runs * runs], axis=0))
    row = lax.broadcasted_iota(jnp.int32, (32, 1024), 0)
    ones = jnp.where(row < 3, 1.0, 0.0)
    parts = [first, first, first, second, second, third]
    table = jnp.concatenate([p.astype(F32) for p in parts] + [ones], axis=0)
    runs_ref[...] = table.T.astype(BF16)
    new = new_ref[:, pl.ds(pl.multiple_of(where_ref[0] * 512, 512), 512)] - 0.5
    aux_ref[...] = jnp.zeros((8, 128), F32)
    row = lax.broadcasted_iota(jnp.int32, (32, 512), 0)
    for block in range(4):
        mine = wide_ref[pl.ds(64 * block + where_ref[1], 1), :]
        column = jnp.broadcast_to(mine, (128, 128)).T
        value = (column[0:16] + column[16:32]) + column[32:48]
        aux_ref[block : block + 1, :] = value[8:9] * LN2
        lscale = value[:8]
        weight = (3.0 * LOG2E * LOG2E) / (lscale * lscale)
        weight = jnp.concatenate([weight] * 4, axis=1)
        scaled = weight * new
        first, second, third = split3(jnp.concatenate([-2.0 * scaled, weight], axis=0))
        square = jnp.broadcast_to(jnp.sum(scaled * new, axis=0, keepdims=True), (32, 512))
        lead, mid, low = [p.astype(F32) for p in split3(square)]
        tail = jnp.where(row == 0, lead, jnp.where(row == 1, mid, jnp.where(row == 2, low, 0.0)))
        new_out_ref[block] = jnp.concatenate(
            [first, second, third, first, second, first, tail.astype(BF16)], axis=0
        )


def prepare(where, basis, design, new_settings):
    return pl.pallas_call(
        prepare_kernel,
        grid=(1,),
        out_shape=(
            jax.ShapeDtypeStruct((1024, 128), BF16),
            jax.ShapeDtypeStruct((4, 128, 512), BF16),
            jax.ShapeDtypeStruct((8, 128), F32),
        ),
        in_specs=[
            SMEM,
            pl.BlockSpec((256, 128), lambda i: (0, CELLS // 128)),
            pl.BlockSpec((8, 1024), lambda i: (0, 0)),
            pl.BlockSpec((8, 2048), lambda i: (0, 0)),
        ],
        out_specs=(
            pl.BlockSpec((1024, 128), lambda i: (0, 0)),
            pl.BlockSpec((4, 128, 512), lambda i: (0, 0, 0)),
            pl.BlockSpec((8, 128), lambda i: (0, 0)),
        ),
        scratch_shapes=[pltpu.VMEM((256, 128), F32)],
        compiler_params=params(16),
        cost_estimate=pl.CostEstimate(flops=1 << 24, bytes_accessed=1 << 20, transcendentals=0),
    )(where, basis, design, new_settings)


def predict_kernel(runs_ref, new_ref, pieces_ref, aux_ref, out_ref, spread_ref, pred_ref):
    both = jnp.sum(pieces_ref[...], axis=0)
    parts = [p.astype(F32) for p in split3(both)]
    table = jnp.concatenate(parts + [jnp.zeros((32, 128), F32)], axis=0).T.astype(BF16)
    row = lax.broadcasted_iota(jnp.int32, (128, 512), 0)
    col = lax.broadcasted_iota(jnp.int32, (128, 512), 1)
    for tile in range(8):
        pick = ((row % 32 == 8 * (col // 128) + tile) & (row < 96)).astype(BF16)
        spread_ref[128 * tile : 128 * tile + 128, :] = jnp.dot(
            table, pick, preferred_element_type=F32
        )

    for block in range(4):
        acc = [jnp.zeros((8, 128), F32)] * 4
        for chunk in range(16):
            rows = slice(64 * chunk, 64 * chunk + 64)
            weight = spread_ref[rows, 128 * block : 128 * block + 128]
            sq = jnp.dot(runs_ref[rows], new_ref[block], preferred_element_type=F32)
            sq = jnp.maximum(sq, 1e-30)
            dist = sq * lax.rsqrt(sq)
            values = (LOG2E + dist) * jnp.exp2(-dist)
            for tile in range(4):
                prod = values[:, 128 * tile : 128 * tile + 128] * weight
                acc[tile] = acc[tile] + jnp.sum(prod.reshape(8, 8, 128), axis=0)
        for tile in range(4):
            where = (tile // 2) * 8 + 2 * block + tile % 2
            total = jnp.sum(acc[tile], axis=0, keepdims=True)
            pred_ref[where : where + 1, :] = total * aux_ref[block : block + 1, :]

    tile = pred_ref[...].astype(BF16).reshape(1, 2, 8, 128)
    out_ref[...] = jnp.broadcast_to(tile, (64, 2, 8, 128))


def predict(runs_feat, new_feat, pieces, aux):
    return pl.pallas_call(
        predict_kernel,
        out_shape=jax.ShapeDtypeStruct((64, 2, 8, 128), BF16),
        in_specs=[VMEM] * 4,
        out_specs=VMEM,
        scratch_shapes=[pltpu.VMEM((1024, 512), F32), pltpu.VMEM((16, 128), F32)],
        compiler_params=params(16),
        cost_estimate=pl.CostEstimate(
            flops=1 << 28, bytes_accessed=1 << 20, transcendentals=1 << 22
        ),
    )(runs_feat, new_feat, pieces, aux)


def rebuild_kernel(scale, where_ref, pred_ref, *refs):
    own_ref, other_ref, out_ref, wide_ref, lhs_ref = refs

    @pl.when(pl.program_id(0) == 0)
    def _():
        wide_ref[...] = pred_ref[...].astype(F32).reshape(1024, 128)
        zl = where_ref[2]
        for side, which in enumerate((zl, 1 - zl)):
            rows = []
            for block in range(4):
                first = 8 * which + 2 * block
                for core in range(2):
                    halves = [
                        wide_ref[pl.ds(16 * core + first + half, 32, stride=32), :]
                        for half in range(2)
                    ]
                    rows.append(jnp.concatenate(halves, axis=1))
            table = jnp.concatenate(rows, axis=0)
            lhs_ref[:, 256 * side : 256 * side + 256] = table.T.astype(BF16)

    total = jnp.dot(lhs_ref[:, :256], own_ref[...], preferred_element_type=F32)
    total = total + jnp.dot(lhs_ref[:, 256:], other_ref[...], preferred_element_type=F32)
    out_ref[...] = (total * scale).astype(BF16)


def rebuild(where, pred, own, other, scale):
    def body(*refs):
        rebuild_kernel(scale, *refs)

    width = 512
    return pl.pallas_call(
        body,
        grid=(CELLS // width,),
        out_shape=jax.ShapeDtypeStruct((256, CELLS), BF16),
        in_specs=[
            SMEM,
            pl.BlockSpec((64, 2, 8, 128), lambda i: (0, 0, 0, 0)),
            *[pl.BlockSpec((256, width), lambda i: (0, i))] * 2,
        ],
        out_specs=pl.BlockSpec((256, width), lambda i: (0, i)),
        scratch_shapes=[pltpu.VMEM((1024, 128), F32), pltpu.VMEM((256, 512), BF16)],
        compiler_params=params(16),
        cost_estimate=pl.CostEstimate(flops=1 << 29, bytes_accessed=3 << 20, transcendentals=0),
    )(where, pred, own, other)


def on_device(fields_runs, eof_basis, weights_inv, design, new_settings, lscale, variance):
    zh, core = lax.axis_index("zh"), lax.axis_index("core")
    column = 32 * core + 8 * zh + lax.axis_index("y")
    where = jnp.stack([lax.axis_index("x"), column, lax.axis_index("zl"), 2 * zh + core])
    swap = [(0, 1), (1, 0)]

    fields_other = lax.ppermute(fields_runs, "zl", swap)
    basis = lax.all_to_all(
        pack(eof_basis.T, lscale, variance.reshape(1, 64)), "x", 0, 0, tiled=True
    ).reshape(256, WIDE)
    pair = lax.all_gather(weights_inv.T.astype(BF16), "core", axis=0, tiled=True)
    pair = lax.ppermute(
        pair, ("zh", "x"), [(a * 4 + b, b * 4 + a) for a in range(4) for b in range(4)]
    )

    sent = project(where, fields_runs, fields_other, basis, pair, 1.0 / math.sqrt(131072))
    parts = lax.all_to_all(sent, GRID, 0, 0, tiled=True)

    runs_feat, new_feat, aux = prepare(where, basis, design, new_settings)
    basis_other = lax.ppermute(basis, "zl", swap)

    pieces = lax.all_to_all(weights(parts), ("x", "core"), 0, 0, tiled=True)
    pred = predict(runs_feat, new_feat, pieces, aux)
    pred = lax.all_to_all(pred.reshape(128, 8, 128), GRID + ("zl",), 0, 0, tiled=True)
    return rebuild(
        where, pred.reshape(64, 2, 8, 128), basis, basis_other, 1.0 / math.sqrt(512)
    )


def solution(mesh):
    fine = Mesh(mesh.devices.reshape(4, 8, 2, 4, 2), GRID + COMP)
    placed = (
        P(COMP, GRID),
        P(GRID, COMP),
        P(None, GRID),
        P(),
        P(),
        P(None, COMP),
        P(COMP),
    )
    return jax.shard_map(
        on_device, mesh=fine, in_specs=placed, out_specs=P(COMP, GRID), check_vma=False
    )
```

```python
import math

import jax
import jax.numpy as jnp
from jax import lax
from jax.experimental import pallas as pl
from jax.experimental.pallas import tpu as pltpu
from jax.sharding import Mesh, PartitionSpec as P

GRID = ("zh", "y", "core")
COMP = ("x", "zl")
LOG2E = 1.4426950408889634
LN2 = 0.6931471805599453
F32 = jnp.float32
BF16 = jnp.bfloat16
HIGHEST = lax.Precision.HIGHEST
VMEM = pl.BlockSpec(memory_space=pltpu.VMEM)
SMEM = pl.BlockSpec(memory_space=pltpu.SMEM)
CELLS = 2048
WIDE = CELLS + 128


def params(mib):
    return pltpu.CompilerParams(vmem_limit_bytes=mib << 20)


def split3(value):
    first = value.astype(BF16)
    rest = value - first.astype(F32)
    second = rest.astype(BF16)
    third = (rest - second.astype(F32)).astype(BF16)
    return first, second, third


def pack_kernel(basis_ref, lscale_ref, variance_ref, out_ref):
    row = lax.broadcasted_iota(jnp.int32, (8, 64), 0)
    tail = jnp.where(row == 0, jnp.broadcast_to(variance_ref[...], (8, 64)), 0.0)
    value = jnp.concatenate([lscale_ref[...], tail], axis=0)
    pieces = jnp.concatenate([part.astype(F32) for part in split3(value)], axis=0)
    pieces = jnp.concatenate([pieces, jnp.zeros((80, 64), F32)], axis=0)
    side = jnp.concatenate([pieces, jnp.zeros((128, 64), F32)], axis=1).T[:64].astype(BF16)
    basis = basis_ref[...]
    for peer in range(4):
        out_ref[peer, :, :CELLS] = basis
        out_ref[peer, :, CELLS:] = side


def pack(basis, lscale, variance):
    return pl.pallas_call(
        pack_kernel,
        out_shape=jax.ShapeDtypeStruct((4, 64, WIDE), BF16),
        in_specs=[VMEM] * 3,
        out_specs=VMEM,
        compiler_params=params(60),
        cost_estimate=pl.CostEstimate(flops=0, bytes_accessed=5 << 18, transcendentals=0),
    )(basis, lscale, variance)


def project_kernel(scale, where_ref, own_ref, other_ref, basis_ref, mine_ref, theirs_ref, runs_ref):
    zl = where_ref[2]
    core = where_ref[4]
    for half, fields_ref in ((zl, own_ref), (1 - zl, other_ref)):
        for y in range(4):
            for side in range(2):
                first = 128 * lax.rem(side + core, 2) + 64 * half + 16 * y
                from_row = 32 * y + 16 * side
                runs_ref[pl.ds(pl.multiple_of(first, 16), 16), :] = fields_ref[
                    from_row : from_row + 16
                ]
    part = lax.dot_general(
        basis_ref[:, :CELLS], runs_ref[...], (((1,), (1,)), ((), ())), preferred_element_type=F32
    )
    mine_ref[...] = part[:, :128] * scale
    theirs_ref[...] = part[:, 128:] * scale


def project(where, own, other, basis, scale):
    def body(*refs):
        project_kernel(scale, *refs)

    half = jax.ShapeDtypeStruct((256, 128), F32)
    return pl.pallas_call(
        body,
        out_shape=(half, half),
        in_specs=[SMEM] + [VMEM] * 3,
        out_specs=(VMEM, VMEM),
        scratch_shapes=[pltpu.VMEM((256, CELLS), BF16)],
        compiler_params=params(16),
        cost_estimate=pl.CostEstimate(flops=1 << 28, bytes_accessed=1 << 21, transcendentals=0),
    )(where, own, other, basis)


def slots_kernel(where_ref, mine_ref, theirs_ref, block_ref, out_ref, wide_ref):
    part = mine_ref[...] + theirs_ref[1 - where_ref[4]]
    high = part.astype(BF16).astype(F32)
    low = part - high
    for block in range(4):
        for core in range(2):
            first = 64 * block + 32 * core
            row = 4 * core + block
            wide_ref[pl.ds(row, 32, stride=16), :] = high[first : first + 32]
            wide_ref[pl.ds(row + 8, 32, stride=16), :] = low[first : first + 32]
    out_ref[:, :16, :] = wide_ref[...].astype(BF16).reshape(32, 16, 128)
    for side in range(2):
        lanes = pl.ds(pl.multiple_of(256 * where_ref[3] + 128 * side, 128), 128)
        piece = block_ref[:, lanes]
        for chip in range(32):
            out_ref[chip, 16 + 16 * side : 32 + 16 * side, :] = piece


def slots(where, mine, theirs, block):
    return pl.pallas_call(
        slots_kernel,
        out_shape=jax.ShapeDtypeStruct((32, 48, 128), BF16),
        in_specs=[SMEM] + [VMEM] * 3,
        out_specs=VMEM,
        scratch_shapes=[pltpu.VMEM((512, 128), F32)],
        compiler_params=params(16),
        cost_estimate=pl.CostEstimate(flops=1 << 20, bytes_accessed=1 << 20, transcendentals=0),
    )(where, mine, theirs, block)


def weights_kernel(parts_ref, out_ref, winv_ref):
    for chip in range(32):
        zh, y = chip // 8, chip % 8
        for side in range(2):
            winv_ref[16 * y : 16 * y + 16, 256 * zh + 128 * side : 256 * zh + 128 * side + 128] = (
                parts_ref[chip, 16 + 16 * side : 32 + 16 * side, :]
            )
    both = jnp.sum(parts_ref[:, :16, :].astype(F32), axis=0)
    coef = both[:8] + both[8:]
    rows = jnp.concatenate(
        [p.astype(F32) for p in split3(coef)] + [jnp.zeros((8, 128), F32)], axis=0
    ).astype(BF16)
    full = jnp.dot(rows, winv_ref[...], preferred_element_type=F32)
    full = (full[16:24] + full[8:16]) + full[:8]
    for core in range(2):
        for block in range(4):
            for tile in range(8):
                piece = full[4 * core + block : 4 * core + block + 1, 128 * tile : 128 * tile + 128]
                for peer in range(4):
                    row = 8 * block + tile
                    out_ref[2 * peer + core, row : row + 1, :] = piece


def weights(parts):
    return pl.pallas_call(
        weights_kernel,
        out_shape=jax.ShapeDtypeStruct((8, 32, 128), F32),
        in_specs=[VMEM],
        out_specs=VMEM,
        scratch_shapes=[pltpu.VMEM((128, 1024), BF16)],
        compiler_params=params(16),
        cost_estimate=pl.CostEstimate(flops=1 << 23, bytes_accessed=1 << 20, transcendentals=0),
    )(parts)


def prepare_kernel(where_ref, side_ref, design_ref, new_ref, runs_ref, new_out_ref, aux_ref, wide_ref):
    wide_ref[...] = side_ref[...].astype(F32)
    runs = design_ref[...] - 0.5
    first, second, third = split3(jnp.concatenate([runs, runs * runs], axis=0))
    row = lax.broadcasted_iota(jnp.int32, (32, 1024), 0)
    ones = jnp.where(row < 3, 1.0, 0.0)
    parts = [first, first, first, second, second, third]
    table = jnp.concatenate([p.astype(F32) for p in parts] + [ones], axis=0)
    runs_ref[...] = table.T.astype(BF16)
    new = new_ref[:, pl.ds(pl.multiple_of(where_ref[0] * 512, 512), 512)] - 0.5
    aux_ref[...] = jnp.zeros((8, 128), F32)
    row = lax.broadcasted_iota(jnp.int32, (32, 512), 0)
    for block in range(4):
        mine = wide_ref[pl.ds(64 * block + where_ref[1], 1), :]
        column = jnp.broadcast_to(mine, (128, 128)).T
        value = (column[0:16] + column[16:32]) + column[32:48]
        aux_ref[block : block + 1, :] = value[8:9] * LN2
        lscale = value[:8]
        weight = (3.0 * LOG2E * LOG2E) / (lscale * lscale)
        weight = jnp.concatenate([weight] * 4, axis=1)
        scaled = weight * new
        first, second, third = split3(jnp.concatenate([-2.0 * scaled, weight], axis=0))
        square = jnp.broadcast_to(jnp.sum(scaled * new, axis=0, keepdims=True), (32, 512))
        lead, mid, low = [p.astype(F32) for p in split3(square)]
        tail = jnp.where(row == 0, lead, jnp.where(row == 1, mid, jnp.where(row == 2, low, 0.0)))
        new_out_ref[block] = jnp.concatenate(
            [first, second, third, first, second, first, tail.astype(BF16)], axis=0
        )


def prepare(where, basis, design, new_settings):
    return pl.pallas_call(
        prepare_kernel,
        grid=(1,),
        out_shape=(
            jax.ShapeDtypeStruct((1024, 128), BF16),
            jax.ShapeDtypeStruct((4, 128, 512), BF16),
            jax.ShapeDtypeStruct((8, 128), F32),
        ),
        in_specs=[
            SMEM,
            pl.BlockSpec((256, 128), lambda i: (0, CELLS // 128)),
            pl.BlockSpec((8, 1024), lambda i: (0, 0)),
            pl.BlockSpec((8, 2048), lambda i: (0, 0)),
        ],
        out_specs=(
            pl.BlockSpec((1024, 128), lambda i: (0, 0)),
            pl.BlockSpec((4, 128, 512), lambda i: (0, 0, 0)),
            pl.BlockSpec((8, 128), lambda i: (0, 0)),
        ),
        scratch_shapes=[pltpu.VMEM((256, 128), F32)],
        compiler_params=params(16),
        cost_estimate=pl.CostEstimate(flops=1 << 24, bytes_accessed=1 << 20, transcendentals=0),
    )(where, basis, design, new_settings)


def predict_kernel(runs_ref, new_ref, pieces_ref, aux_ref, out_ref, spread_ref, pred_ref):
    both = jnp.sum(pieces_ref[...], axis=0)
    parts = [p.astype(F32) for p in split3(both)]
    table = jnp.concatenate(parts + [jnp.zeros((32, 128), F32)], axis=0).T.astype(BF16)
    row = lax.broadcasted_iota(jnp.int32, (128, 512), 0)
    col = lax.broadcasted_iota(jnp.int32, (128, 512), 1)
    for tile in range(8):
        pick = ((row % 32 == 8 * (col // 128) + tile) & (row < 96)).astype(BF16)
        spread_ref[128 * tile : 128 * tile + 128, :] = jnp.dot(
            table, pick, preferred_element_type=F32
        )

    for block in range(4):
        acc = [jnp.zeros((8, 128), F32)] * 4
        for chunk in range(16):
            rows = slice(64 * chunk, 64 * chunk + 64)
            weight = spread_ref[rows, 128 * block : 128 * block + 128]
            sq = jnp.dot(runs_ref[rows], new_ref[block], preferred_element_type=F32)
            sq = jnp.maximum(sq, 1e-30)
            dist = sq * lax.rsqrt(sq)
            values = (LOG2E + dist) * jnp.exp2(-dist)
            for tile in range(4):
                prod = values[:, 128 * tile : 128 * tile + 128] * weight
                acc[tile] = acc[tile] + jnp.sum(prod.reshape(8, 8, 128), axis=0)
        for tile in range(4):
            where = (tile // 2) * 8 + 2 * block + tile % 2
            total = jnp.sum(acc[tile], axis=0, keepdims=True)
            pred_ref[where : where + 1, :] = total * aux_ref[block : block + 1, :]

    tile = pred_ref[...].astype(BF16).reshape(1, 2, 8, 128)
    out_ref[...] = jnp.broadcast_to(tile, (32, 2, 8, 128))


def predict(runs_feat, new_feat, pieces, aux):
    return pl.pallas_call(
        predict_kernel,
        out_shape=jax.ShapeDtypeStruct((32, 2, 8, 128), BF16),
        in_specs=[VMEM] * 4,
        out_specs=VMEM,
        scratch_shapes=[pltpu.VMEM((1024, 512), F32), pltpu.VMEM((16, 128), F32)],
        compiler_params=params(16),
        cost_estimate=pl.CostEstimate(
            flops=1 << 28, bytes_accessed=1 << 20, transcendentals=1 << 22
        ),
    )(runs_feat, new_feat, pieces, aux)


def rebuild_kernel(
    scale, where_ref, pred_ref, own_ref, other_ref, out_ref, wide_ref, lhs_ref, done_ref, sems
):
    wide_ref[...] = pred_ref[...].astype(F32).reshape(1024, 128)
    zl = where_ref[2]
    for side, which in enumerate((zl, 1 - zl)):
        rows = []
        for block in range(4):
            first = 8 * which + 2 * block
            for core in range(2):
                halves = [
                    wide_ref[pl.ds(512 * core + first + half, 32, stride=16), :]
                    for half in range(2)
                ]
                rows.append(jnp.concatenate(halves, axis=1))
        table = jnp.concatenate(rows, axis=0)
        lhs_ref[:, 256 * side : 256 * side + 256] = table.T.astype(BF16)

    copies = []
    for chunk in range(4):
        cells = slice(512 * chunk, 512 * chunk + 512)
        total = jnp.dot(lhs_ref[:, :256], own_ref[:, cells], preferred_element_type=F32)
        total = total + jnp.dot(lhs_ref[:, 256:], other_ref[:, cells], preferred_element_type=F32)
        done_ref[:, cells] = (total * scale).astype(BF16)
        copy = pltpu.make_async_copy(done_ref.at[:, cells], out_ref.at[:, cells], sems.at[chunk])
        copy.start()
        copies.append(copy)
    for copy in copies:
        copy.wait()


def rebuild(where, pred, own, other, scale):
    def body(*refs):
        rebuild_kernel(scale, *refs)

    return pl.pallas_call(
        body,
        out_shape=jax.ShapeDtypeStruct((256, CELLS), BF16),
        in_specs=[SMEM] + [VMEM] * 3,
        out_specs=pl.BlockSpec(memory_space=pl.ANY),
        scratch_shapes=[
            pltpu.VMEM((1024, 128), F32),
            pltpu.VMEM((256, 512), BF16),
            pltpu.VMEM((256, CELLS), BF16),
            pltpu.SemaphoreType.DMA((4,)),
        ],
        compiler_params=params(16),
        cost_estimate=pl.CostEstimate(flops=1 << 29, bytes_accessed=3 << 20, transcendentals=0),
    )(where, pred, own, other)


def on_device(fields_runs, eof_basis, weights_inv, design, new_settings, lscale, variance):
    zh, core = lax.axis_index("zh"), lax.axis_index("core")
    column = 32 * core + 8 * zh + lax.axis_index("y")
    where = jnp.stack([lax.axis_index("x"), column, lax.axis_index("zl"), zh, core])
    swap = [(0, 1), (1, 0)]

    fields_other = lax.ppermute(fields_runs, "zl", swap)
    basis = lax.all_to_all(
        pack(eof_basis.T, lscale, variance.reshape(1, 64)), "x", 0, 0, tiled=True
    ).reshape(256, WIDE)
    block = lax.ppermute(
        weights_inv.T.astype(BF16),
        ("zh", "x"),
        [(a * 4 + b, b * 4 + a) for a in range(4) for b in range(4)],
    )

    mine, theirs = project(where, fields_runs, fields_other, basis, 1.0 / math.sqrt(131072))
    theirs = lax.all_gather(theirs, "core", axis=0)
    parts = lax.all_to_all(slots(where, mine, theirs, block), ("zh", "y"), 0, 0, tiled=True)

    runs_feat, new_feat, aux = prepare(where, basis, design, new_settings)
    basis_other = lax.ppermute(basis, "zl", swap)

    pieces = lax.all_to_all(weights(parts), ("x", "core"), 0, 0, tiled=True)
    pred = predict(runs_feat, new_feat, pieces, aux)
    pred = lax.all_to_all(pred.reshape(64, 8, 128), ("zh", "y", "zl"), 0, 0, tiled=True)
    pred = lax.all_gather(pred, "core", axis=0, tiled=True)
    return rebuild(
        where, pred.reshape(64, 2, 8, 128), basis, basis_other, 1.0 / math.sqrt(512)
    )


def solution(mesh):
    fine = Mesh(mesh.devices.reshape(4, 8, 2, 4, 2), GRID + COMP)
    placed = (
        P(COMP, GRID),
        P(GRID, COMP),
        P(None, GRID),
        P(),
        P(),
        P(None, COMP),
        P(COMP),
    )
    return jax.shard_map(
        on_device, mesh=fine, in_specs=placed, out_specs=P(COMP, GRID), check_vma=False
    )
```

```python
import math

import jax
import jax.numpy as jnp
from jax import lax
from jax.experimental import pallas as pl
from jax.experimental.pallas import tpu as pltpu
from jax.sharding import Mesh, PartitionSpec as P

GRID = ("zh", "y", "core")
COMP = ("x", "zl")
LOG2E = 1.4426950408889634
LN2 = 0.6931471805599453
F32 = jnp.float32
BF16 = jnp.bfloat16
HIGHEST = lax.Precision.HIGHEST
VMEM = pl.BlockSpec(memory_space=pltpu.VMEM)
SMEM = pl.BlockSpec(memory_space=pltpu.SMEM)
CELLS = 2048
WIDE = CELLS + 128


def params(mib):
    return pltpu.CompilerParams(vmem_limit_bytes=mib << 20)


def split3(value):
    first = value.astype(BF16)
    rest = value - first.astype(F32)
    second = rest.astype(BF16)
    third = (rest - second.astype(F32)).astype(BF16)
    return first, second, third


def pack_kernel(basis_ref, lscale_ref, variance_ref, out_ref):
    row = lax.broadcasted_iota(jnp.int32, (8, 64), 0)
    tail = jnp.where(row == 0, jnp.broadcast_to(variance_ref[...], (8, 64)), 0.0)
    value = jnp.concatenate([lscale_ref[...], tail], axis=0)
    pieces = jnp.concatenate([part.astype(F32) for part in split3(value)], axis=0)
    pieces = jnp.concatenate([pieces, jnp.zeros((80, 64), F32)], axis=0)
    side = jnp.concatenate([pieces, jnp.zeros((128, 64), F32)], axis=1).T[:64].astype(BF16)
    basis = basis_ref[...]
    for peer in range(4):
        out_ref[peer, :, :CELLS] = basis
        out_ref[peer, :, CELLS:] = side


def pack(basis, lscale, variance):
    return pl.pallas_call(
        pack_kernel,
        out_shape=jax.ShapeDtypeStruct((4, 64, WIDE), BF16),
        in_specs=[VMEM] * 3,
        out_specs=VMEM,
        compiler_params=params(60),
        cost_estimate=pl.CostEstimate(flops=0, bytes_accessed=5 << 18, transcendentals=0),
    )(basis, lscale, variance)


def project_kernel(scale, where_ref, own_ref, other_ref, basis_ref, mine_ref, theirs_ref, runs_ref):
    zl = where_ref[2]
    core = where_ref[4]
    for half, fields_ref in ((zl, own_ref), (1 - zl, other_ref)):
        for y in range(4):
            for side in range(2):
                first = 128 * lax.rem(side + core, 2) + 64 * half + 16 * y
                from_row = 32 * y + 16 * side
                runs_ref[pl.ds(pl.multiple_of(first, 16), 16), :] = fields_ref[
                    from_row : from_row + 16
                ]
    part = lax.dot_general(
        basis_ref[:, :CELLS], runs_ref[...], (((1,), (1,)), ((), ())), preferred_element_type=F32
    )
    mine_ref[...] = part[:, :128] * scale
    theirs_ref[...] = part[:, 128:] * scale


def project(where, own, other, basis, scale):
    def body(*refs):
        project_kernel(scale, *refs)

    half = jax.ShapeDtypeStruct((256, 128), F32)
    return pl.pallas_call(
        body,
        out_shape=(half, half),
        in_specs=[SMEM] + [VMEM] * 3,
        out_specs=(VMEM, VMEM),
        scratch_shapes=[pltpu.VMEM((256, CELLS), BF16)],
        compiler_params=params(16),
        cost_estimate=pl.CostEstimate(flops=1 << 28, bytes_accessed=1 << 21, transcendentals=0),
    )(where, own, other, basis)


def slots_kernel(where_ref, mine_ref, theirs_ref, block_ref, out_ref, wide_ref):
    part = mine_ref[...] + theirs_ref[1 - where_ref[4]]
    high = part.astype(BF16).astype(F32)
    low = part - high
    for block in range(4):
        for core in range(2):
            first = 64 * block + 32 * core
            row = 4 * core + block
            wide_ref[pl.ds(row, 32, stride=16), :] = high[first : first + 32]
            wide_ref[pl.ds(row + 8, 32, stride=16), :] = low[first : first + 32]
    out_ref[:, :16, :] = wide_ref[...].astype(BF16).reshape(32, 16, 128)
    for side in range(2):
        lanes = pl.ds(pl.multiple_of(256 * where_ref[3] + 128 * side, 128), 128)
        piece = block_ref[:, lanes]
        for chip in range(32):
            out_ref[chip, 16 + 16 * side : 32 + 16 * side, :] = piece


def slots(where, mine, theirs, block):
    return pl.pallas_call(
        slots_kernel,
        out_shape=jax.ShapeDtypeStruct((32, 48, 128), BF16),
        in_specs=[SMEM] + [VMEM] * 3,
        out_specs=VMEM,
        scratch_shapes=[pltpu.VMEM((512, 128), F32)],
        compiler_params=params(16),
        cost_estimate=pl.CostEstimate(flops=1 << 20, bytes_accessed=1 << 20, transcendentals=0),
    )(where, mine, theirs, block)


def weights_kernel(parts_ref, after_ref, out_ref, winv_ref):
    for chip in range(32):
        zh, y = chip // 8, chip % 8
        for side in range(2):
            winv_ref[16 * y : 16 * y + 16, 256 * zh + 128 * side : 256 * zh + 128 * side + 128] = (
                parts_ref[chip, 16 + 16 * side : 32 + 16 * side, :]
            )
    both = jnp.sum(parts_ref[:, :16, :].astype(F32), axis=0)
    coef = both[:8] + both[8:]
    rows = jnp.concatenate(
        [p.astype(F32) for p in split3(coef)] + [jnp.zeros((8, 128), F32)], axis=0
    ).astype(BF16)
    full = jnp.dot(rows, winv_ref[...], preferred_element_type=F32)
    full = (full[16:24] + full[8:16]) + full[:8]
    for core in range(2):
        for block in range(4):
            for tile in range(8):
                piece = full[4 * core + block : 4 * core + block + 1, 128 * tile : 128 * tile + 128]
                for peer in range(4):
                    row = 8 * block + tile
                    out_ref[2 * peer + core, row : row + 1, :] = piece


def weights(parts, after):
    return pl.pallas_call(
        weights_kernel,
        out_shape=jax.ShapeDtypeStruct((8, 32, 128), F32),
        in_specs=[VMEM, pl.BlockSpec(memory_space=pl.ANY)],
        out_specs=VMEM,
        scratch_shapes=[pltpu.VMEM((128, 1024), BF16)],
        compiler_params=params(16),
        cost_estimate=pl.CostEstimate(flops=1 << 23, bytes_accessed=1 << 20, transcendentals=0),
    )(parts, after)


def prepare_kernel(where_ref, side_ref, design_ref, new_ref, runs_ref, new_out_ref, aux_ref, wide_ref):
    wide_ref[...] = side_ref[...].astype(F32)
    runs = design_ref[...] - 0.5
    first, second, third = split3(jnp.concatenate([runs, runs * runs], axis=0))
    row = lax.broadcasted_iota(jnp.int32, (32, 1024), 0)
    ones = jnp.where(row < 3, 1.0, 0.0)
    parts = [first, first, first, second, second, third]
    table = jnp.concatenate([p.astype(F32) for p in parts] + [ones], axis=0)
    runs_ref[...] = table.T.astype(BF16)
    new = new_ref[:, pl.ds(pl.multiple_of(where_ref[0] * 512, 512), 512)] - 0.5
    aux_ref[...] = jnp.zeros((8, 128), F32)
    row = lax.broadcasted_iota(jnp.int32, (32, 512), 0)
    for block in range(4):
        mine = wide_ref[pl.ds(64 * block + where_ref[1], 1), :]
        column = jnp.broadcast_to(mine, (128, 128)).T
        value = (column[0:16] + column[16:32]) + column[32:48]
        aux_ref[block : block + 1, :] = value[8:9] * LN2
        lscale = value[:8]
        weight = (3.0 * LOG2E * LOG2E) / (lscale * lscale)
        weight = jnp.concatenate([weight] * 4, axis=1)
        scaled = weight * new
        first, second, third = split3(jnp.concatenate([-2.0 * scaled, weight], axis=0))
        square = jnp.broadcast_to(jnp.sum(scaled * new, axis=0, keepdims=True), (32, 512))
        lead, mid, low = [p.astype(F32) for p in split3(square)]
        tail = jnp.where(row == 0, lead, jnp.where(row == 1, mid, jnp.where(row == 2, low, 0.0)))
        new_out_ref[block] = jnp.concatenate(
            [first, second, third, first, second, first, tail.astype(BF16)], axis=0
        )


def prepare(where, basis, design, new_settings):
    return pl.pallas_call(
        prepare_kernel,
        grid=(1,),
        out_shape=(
            jax.ShapeDtypeStruct((1024, 128), BF16),
            jax.ShapeDtypeStruct((4, 128, 512), BF16),
            jax.ShapeDtypeStruct((8, 128), F32),
        ),
        in_specs=[
            SMEM,
            pl.BlockSpec((256, 128), lambda i: (0, CELLS // 128)),
            pl.BlockSpec((8, 1024), lambda i: (0, 0)),
            pl.BlockSpec((8, 2048), lambda i: (0, 0)),
        ],
        out_specs=(
            pl.BlockSpec((1024, 128), lambda i: (0, 0)),
            pl.BlockSpec((4, 128, 512), lambda i: (0, 0, 0)),
            pl.BlockSpec((8, 128), lambda i: (0, 0)),
        ),
        scratch_shapes=[pltpu.VMEM((256, 128), F32)],
        compiler_params=params(16),
        cost_estimate=pl.CostEstimate(flops=1 << 24, bytes_accessed=1 << 20, transcendentals=0),
    )(where, basis, design, new_settings)


def predict_kernel(runs_ref, new_ref, pieces_ref, aux_ref, out_ref, spread_ref, pred_ref):
    both = jnp.sum(pieces_ref[...], axis=0)
    parts = [p.astype(F32) for p in split3(both)]
    table = jnp.concatenate(parts + [jnp.zeros((32, 128), F32)], axis=0).T
    row = lax.broadcasted_iota(jnp.int32, (128, 512), 0)
    col = lax.broadcasted_iota(jnp.int32, (128, 512), 1)
    pick = ((row % 32 == 8 * (col // 128)) & (row < 96)).astype(BF16)
    for tile in range(8):
        rolled = pltpu.roll(table, (128 - tile) % 128, axis=1).astype(BF16)
        spread_ref[128 * tile : 128 * tile + 128, :] = jnp.dot(
            rolled, pick, preferred_element_type=F32
        )

    for block in range(4):
        acc = [jnp.zeros((8, 128), F32)] * 4
        for chunk in range(16):
            rows = slice(64 * chunk, 64 * chunk + 64)
            weight = spread_ref[rows, 128 * block : 128 * block + 128]
            sq = jnp.dot(runs_ref[rows], new_ref[block], preferred_element_type=F32)
            sq = jnp.maximum(sq, 1e-30)
            dist = sq * lax.rsqrt(sq)
            values = (LOG2E + dist) * jnp.exp2(-dist)
            for tile in range(4):
                prod = values[:, 128 * tile : 128 * tile + 128] * weight
                acc[tile] = acc[tile] + jnp.sum(prod.reshape(8, 8, 128), axis=0)
        for tile in range(4):
            where = (tile // 2) * 8 + 2 * block + tile % 2
            total = jnp.sum(acc[tile], axis=0, keepdims=True)
            pred_ref[where : where + 1, :] = total * aux_ref[block : block + 1, :]

    tile = pred_ref[...].astype(BF16).reshape(1, 2, 8, 128)
    out_ref[...] = jnp.broadcast_to(tile, (32, 2, 8, 128))


def predict(runs_feat, new_feat, pieces, aux):
    return pl.pallas_call(
        predict_kernel,
        out_shape=jax.ShapeDtypeStruct((32, 2, 8, 128), BF16),
        in_specs=[VMEM] * 4,
        out_specs=VMEM,
        scratch_shapes=[pltpu.VMEM((1024, 512), F32), pltpu.VMEM((16, 128), F32)],
        compiler_params=params(16),
        cost_estimate=pl.CostEstimate(
            flops=1 << 28, bytes_accessed=1 << 20, transcendentals=1 << 22
        ),
    )(runs_feat, new_feat, pieces, aux)


def rebuild_kernel(
    scale, where_ref, pred_ref, own_ref, other_ref, out_ref, wide_ref, lhs_ref, done_ref, sems
):
    wide_ref[...] = pred_ref[...].astype(F32).reshape(1024, 128)
    zl = where_ref[2]
    for side, which in enumerate((zl, 1 - zl)):
        rows = []
        for block in range(4):
            first = 8 * which + 2 * block
            for core in range(2):
                halves = [
                    wide_ref[pl.ds(512 * core + first + half, 32, stride=16), :]
                    for half in range(2)
                ]
                rows.append(jnp.concatenate(halves, axis=1))
        table = jnp.concatenate(rows, axis=0)
        lhs_ref[:, 256 * side : 256 * side + 256] = table.T.astype(BF16)

    copies = []
    for chunk in range(4):
        cells = slice(512 * chunk, 512 * chunk + 512)
        total = jnp.dot(lhs_ref[:, :256], own_ref[:, cells], preferred_element_type=F32)
        total = total + jnp.dot(lhs_ref[:, 256:], other_ref[:, cells], preferred_element_type=F32)
        done_ref[:, cells] = (total * scale).astype(BF16)
        copy = pltpu.make_async_copy(done_ref.at[:, cells], out_ref.at[:, cells], sems.at[chunk])
        copy.start()
        copies.append(copy)
    for copy in copies:
        copy.wait()


def rebuild(where, pred, own, other, scale):
    def body(*refs):
        rebuild_kernel(scale, *refs)

    return pl.pallas_call(
        body,
        out_shape=jax.ShapeDtypeStruct((256, CELLS), BF16),
        in_specs=[SMEM] + [VMEM] * 3,
        out_specs=pl.BlockSpec(memory_space=pl.ANY),
        scratch_shapes=[
            pltpu.VMEM((1024, 128), F32),
            pltpu.VMEM((256, 512), BF16),
            pltpu.VMEM((256, CELLS), BF16),
            pltpu.SemaphoreType.DMA((4,)),
        ],
        compiler_params=params(16),
        cost_estimate=pl.CostEstimate(flops=1 << 29, bytes_accessed=3 << 20, transcendentals=0),
    )(where, pred, own, other)


def on_device(fields_runs, eof_basis, weights_inv, design, new_settings, lscale, variance):
    zh, core = lax.axis_index("zh"), lax.axis_index("core")
    column = 32 * core + 8 * zh + lax.axis_index("y")
    where = jnp.stack([lax.axis_index("x"), column, lax.axis_index("zl"), zh, core])
    swap = [(0, 1), (1, 0)]

    fields_other = lax.ppermute(fields_runs, "zl", swap)
    basis = lax.all_to_all(
        pack(eof_basis.T, lscale, variance.reshape(1, 64)), "x", 0, 0, tiled=True
    ).reshape(256, WIDE)
    block = lax.ppermute(
        weights_inv.T.astype(BF16),
        ("zh", "x"),
        [(a * 4 + b, b * 4 + a) for a in range(4) for b in range(4)],
    )

    mine, theirs = project(where, fields_runs, fields_other, basis, 1.0 / math.sqrt(131072))
    theirs = lax.all_gather(theirs, "core", axis=0)
    parts = lax.all_to_all(slots(where, mine, theirs, block), ("zh", "y"), 0, 0, tiled=True)

    runs_feat, new_feat, aux = prepare(where, basis, design, new_settings)
    basis_other = lax.ppermute(basis, "zl", swap)

    pieces = lax.all_to_all(weights(parts, aux), ("x", "core"), 0, 0, tiled=True)
    pred = predict(runs_feat, new_feat, pieces, aux)
    pred = lax.all_to_all(pred.reshape(64, 8, 128), ("zh", "y", "zl"), 0, 0, tiled=True)
    pred = lax.all_gather(pred, "core", axis=0, tiled=True)
    return rebuild(
        where, pred.reshape(64, 2, 8, 128), basis, basis_other, 1.0 / math.sqrt(512)
    )


def solution(mesh):
    fine = Mesh(mesh.devices.reshape(4, 8, 2, 4, 2), GRID + COMP)
    placed = (
        P(COMP, GRID),
        P(GRID, COMP),
        P(None, GRID),
        P(),
        P(),
        P(None, COMP),
        P(COMP),
    )
    return jax.shard_map(
        on_device, mesh=fine, in_specs=placed, out_specs=P(COMP, GRID), check_vma=False
    )
```

```python
import math

import jax
import jax.numpy as jnp
from jax import lax
from jax.experimental import pallas as pl
from jax.experimental.pallas import tpu as pltpu
from jax.sharding import Mesh, PartitionSpec as P

GRID = ("zh", "y", "core")
COMP = ("x", "zl")
LOG2E = 1.4426950408889634
LN2 = 0.6931471805599453
F32 = jnp.float32
BF16 = jnp.bfloat16
HIGHEST = lax.Precision.HIGHEST
VMEM = pl.BlockSpec(memory_space=pltpu.VMEM)
SMEM = pl.BlockSpec(memory_space=pltpu.SMEM)
CELLS = 2048
WIDE = CELLS + 128
BOUNDS = (0, 768, 1280, 1792, 2048)


def params(mib):
    return pltpu.CompilerParams(vmem_limit_bytes=mib << 20)


def split3(value):
    first = value.astype(BF16)
    rest = value - first.astype(F32)
    second = rest.astype(BF16)
    third = (rest - second.astype(F32)).astype(BF16)
    return first, second, third


def pack_kernel(basis_ref, lscale_ref, variance_ref, out_ref):
    row = lax.broadcasted_iota(jnp.int32, (8, 64), 0)
    tail = jnp.where(row == 0, jnp.broadcast_to(variance_ref[...], (8, 64)), 0.0)
    value = jnp.concatenate([lscale_ref[...], tail], axis=0)
    pieces = jnp.concatenate([part.astype(F32) for part in split3(value)], axis=0)
    pieces = jnp.concatenate([pieces, jnp.zeros((80, 64), F32)], axis=0)
    side = jnp.concatenate([pieces, jnp.zeros((128, 64), F32)], axis=1).T[:64].astype(BF16)
    basis = basis_ref[...]
    for peer in range(4):
        out_ref[peer, :, :CELLS] = basis
        out_ref[peer, :, CELLS:] = side


def pack(basis, lscale, variance):
    return pl.pallas_call(
        pack_kernel,
        out_shape=jax.ShapeDtypeStruct((4, 64, WIDE), BF16),
        in_specs=[VMEM] * 3,
        out_specs=VMEM,
        compiler_params=params(60),
        cost_estimate=pl.CostEstimate(flops=0, bytes_accessed=5 << 18, transcendentals=0),
    )(basis, lscale, variance)


def project_kernel(scale, where_ref, own_ref, other_ref, basis_ref, mine_ref, theirs_ref, runs_ref):
    zl = where_ref[2]
    core = where_ref[4]
    for half, fields_ref in ((zl, own_ref), (1 - zl, other_ref)):
        for y in range(4):
            for side in range(2):
                first = 128 * lax.rem(side + core, 2) + 64 * half + 16 * y
                from_row = 32 * y + 16 * side
                runs_ref[pl.ds(pl.multiple_of(first, 16), 16), :] = fields_ref[
                    from_row : from_row + 16
                ]
    part = lax.dot_general(
        basis_ref[:, :CELLS], runs_ref[...], (((1,), (1,)), ((), ())), preferred_element_type=F32
    )
    mine_ref[...] = part[:, :128] * scale
    theirs_ref[...] = part[:, 128:] * scale


def project(where, own, other, basis, scale):
    def body(*refs):
        project_kernel(scale, *refs)

    half = jax.ShapeDtypeStruct((256, 128), F32)
    return pl.pallas_call(
        body,
        out_shape=(half, half),
        in_specs=[SMEM] + [VMEM] * 3,
        out_specs=(VMEM, VMEM),
        scratch_shapes=[pltpu.VMEM((256, CELLS), BF16)],
        compiler_params=params(16),
        cost_estimate=pl.CostEstimate(flops=1 << 28, bytes_accessed=1 << 21, transcendentals=0),
    )(where, own, other, basis)


def slots_kernel(where_ref, mine_ref, theirs_ref, block_ref, out_ref, held_ref, wide_ref, sems):
    for side in range(2):
        lanes = pl.ds(pl.multiple_of(256 * where_ref[3] + 128 * side, 128), 128)
        piece = block_ref[:, lanes]
        for chip in range(32):
            held_ref[chip, 16 + 16 * side : 32 + 16 * side, :] = piece
    lower = pltpu.make_async_copy(held_ref.at[:, 16:, :], out_ref.at[:, 16:, :], sems.at[0])
    lower.start()
    part = mine_ref[...] + theirs_ref[1 - where_ref[4]]
    high = part.astype(BF16).astype(F32)
    low = part - high
    for block in range(4):
        for core in range(2):
            first = 64 * block + 32 * core
            row = 4 * core + block
            wide_ref[pl.ds(row, 32, stride=16), :] = high[first : first + 32]
            wide_ref[pl.ds(row + 8, 32, stride=16), :] = low[first : first + 32]
    held_ref[:, :16, :] = wide_ref[...].astype(BF16).reshape(32, 16, 128)
    upper = pltpu.make_async_copy(held_ref.at[:, :16, :], out_ref.at[:, :16, :], sems.at[1])
    upper.start()
    lower.wait()
    upper.wait()


def slots(where, mine, theirs, block):
    return pl.pallas_call(
        slots_kernel,
        out_shape=jax.ShapeDtypeStruct((32, 48, 128), BF16),
        in_specs=[SMEM] + [VMEM] * 3,
        out_specs=pl.BlockSpec(memory_space=pl.ANY),
        scratch_shapes=[
            pltpu.VMEM((32, 48, 128), BF16),
            pltpu.VMEM((512, 128), F32),
            pltpu.SemaphoreType.DMA((2,)),
        ],
        compiler_params=params(16),
        cost_estimate=pl.CostEstimate(flops=1 << 20, bytes_accessed=1 << 20, transcendentals=0),
    )(where, mine, theirs, block)


def weights_kernel(parts_ref, after_ref, out_ref, winv_ref):
    for chip in range(32):
        zh, y = chip // 8, chip % 8
        for side in range(2):
            winv_ref[16 * y : 16 * y + 16, 256 * zh + 128 * side : 256 * zh + 128 * side + 128] = (
                parts_ref[chip, 16 + 16 * side : 32 + 16 * side, :]
            )
    both = jnp.sum(parts_ref[:, :16, :].astype(F32), axis=0)
    coef = both[:8] + both[8:]
    rows = jnp.concatenate(
        [p.astype(F32) for p in split3(coef)] + [jnp.zeros((8, 128), F32)], axis=0
    ).astype(BF16)
    full = jnp.dot(rows, winv_ref[...], preferred_element_type=F32)
    full = (full[16:24] + full[8:16]) + full[:8]
    for core in range(2):
        for block in range(4):
            for tile in range(8):
                piece = full[4 * core + block : 4 * core + block + 1, 128 * tile : 128 * tile + 128]
                for peer in range(4):
                    row = 8 * block + tile
                    out_ref[2 * peer + core, row : row + 1, :] = piece


def weights(parts, after):
    return pl.pallas_call(
        weights_kernel,
        out_shape=jax.ShapeDtypeStruct((8, 32, 128), F32),
        in_specs=[VMEM, pl.BlockSpec(memory_space=pl.ANY)],
        out_specs=VMEM,
        scratch_shapes=[pltpu.VMEM((128, 1024), BF16)],
        compiler_params=params(16),
        cost_estimate=pl.CostEstimate(flops=1 << 23, bytes_accessed=1 << 20, transcendentals=0),
    )(parts, after)


def prepare_kernel(where_ref, side_ref, design_ref, new_ref, runs_ref, new_out_ref, aux_ref, wide_ref):
    wide_ref[...] = side_ref[...].astype(F32)
    runs = design_ref[...] - 0.5
    first, second, third = split3(jnp.concatenate([runs, runs * runs], axis=0))
    row = lax.broadcasted_iota(jnp.int32, (32, 1024), 0)
    ones = jnp.where(row < 3, 1.0, 0.0)
    parts = [first, first, first, second, second, third]
    table = jnp.concatenate([p.astype(F32) for p in parts] + [ones], axis=0)
    runs_ref[...] = table.T.astype(BF16)
    new = new_ref[:, pl.ds(pl.multiple_of(where_ref[0] * 512, 512), 512)] - 0.5
    aux_ref[...] = jnp.zeros((8, 128), F32)
    row = lax.broadcasted_iota(jnp.int32, (32, 512), 0)
    for block in range(4):
        mine = wide_ref[pl.ds(64 * block + where_ref[1], 1), :]
        column = jnp.broadcast_to(mine, (128, 128)).T
        value = (column[0:16] + column[16:32]) + column[32:48]
        aux_ref[block : block + 1, :] = value[8:9] * LN2
        lscale = value[:8]
        weight = (3.0 * LOG2E * LOG2E) / (lscale * lscale)
        weight = jnp.concatenate([weight] * 4, axis=1)
        scaled = weight * new
        first, second, third = split3(jnp.concatenate([-2.0 * scaled, weight], axis=0))
        square = jnp.broadcast_to(jnp.sum(scaled * new, axis=0, keepdims=True), (32, 512))
        lead, mid, low = [p.astype(F32) for p in split3(square)]
        tail = jnp.where(row == 0, lead, jnp.where(row == 1, mid, jnp.where(row == 2, low, 0.0)))
        new_out_ref[block] = jnp.concatenate(
            [first, second, third, first, second, first, tail.astype(BF16)], axis=0
        )


def prepare(where, basis, design, new_settings):
    return pl.pallas_call(
        prepare_kernel,
        grid=(1,),
        out_shape=(
            jax.ShapeDtypeStruct((1024, 128), BF16),
            jax.ShapeDtypeStruct((4, 128, 512), BF16),
            jax.ShapeDtypeStruct((8, 128), F32),
        ),
        in_specs=[
            SMEM,
            pl.BlockSpec((256, 128), lambda i: (0, CELLS // 128)),
            pl.BlockSpec((8, 1024), lambda i: (0, 0)),
            pl.BlockSpec((8, 2048), lambda i: (0, 0)),
        ],
        out_specs=(
            pl.BlockSpec((1024, 128), lambda i: (0, 0)),
            pl.BlockSpec((4, 128, 512), lambda i: (0, 0, 0)),
            pl.BlockSpec((8, 128), lambda i: (0, 0)),
        ),
        scratch_shapes=[pltpu.VMEM((256, 128), F32)],
        compiler_params=params(16),
        cost_estimate=pl.CostEstimate(flops=1 << 24, bytes_accessed=1 << 20, transcendentals=0),
    )(where, basis, design, new_settings)


def predict_kernel(runs_ref, new_ref, pieces_ref, aux_ref, out_ref, spread_ref, pred_ref):
    both = jnp.sum(pieces_ref[...], axis=0)
    parts = [p.astype(F32) for p in split3(both)]
    table = jnp.concatenate(parts + [jnp.zeros((32, 128), F32)], axis=0).T
    row = lax.broadcasted_iota(jnp.int32, (128, 512), 0)
    col = lax.broadcasted_iota(jnp.int32, (128, 512), 1)
    pick = ((row % 32 == 8 * (col // 128)) & (row < 96)).astype(BF16)
    for tile in range(8):
        rolled = pltpu.roll(table, (128 - tile) % 128, axis=1).astype(BF16)
        spread_ref[128 * tile : 128 * tile + 128, :] = jnp.dot(
            rolled, pick, preferred_element_type=F32
        )

    for block in range(4):
        acc = [jnp.zeros((8, 128), F32)] * 4
        for chunk in range(16):
            rows = slice(64 * chunk, 64 * chunk + 64)
            weight = spread_ref[rows, 128 * block : 128 * block + 128]
            sq = jnp.dot(runs_ref[rows], new_ref[block], preferred_element_type=F32)
            sq = jnp.maximum(sq, 1e-30)
            dist = sq * lax.rsqrt(sq)
            values = (LOG2E + dist) * jnp.exp2(-dist)
            for tile in range(4):
                prod = values[:, 128 * tile : 128 * tile + 128] * weight
                acc[tile] = acc[tile] + jnp.sum(prod.reshape(8, 8, 128), axis=0)
        for tile in range(4):
            where = (tile // 2) * 8 + 2 * block + tile % 2
            total = jnp.sum(acc[tile], axis=0, keepdims=True)
            pred_ref[where : where + 1, :] = total * aux_ref[block : block + 1, :]

    tile = pred_ref[...].astype(BF16).reshape(1, 2, 8, 128)
    out_ref[...] = jnp.broadcast_to(tile, (32, 2, 8, 128))


def predict(runs_feat, new_feat, pieces, aux):
    return pl.pallas_call(
        predict_kernel,
        out_shape=jax.ShapeDtypeStruct((32, 2, 8, 128), BF16),
        in_specs=[VMEM] * 4,
        out_specs=VMEM,
        scratch_shapes=[pltpu.VMEM((1024, 512), F32), pltpu.VMEM((16, 128), F32)],
        compiler_params=params(16),
        cost_estimate=pl.CostEstimate(
            flops=1 << 28, bytes_accessed=1 << 20, transcendentals=1 << 22
        ),
    )(runs_feat, new_feat, pieces, aux)


def rebuild_kernel(
    scale, where_ref, pred_ref, own_ref, other_ref, out_ref, wide_ref, lhs_ref, done_ref, sems
):
    wide_ref[...] = pred_ref[...].astype(F32).reshape(1024, 128)
    zl = where_ref[2]
    for side, which in enumerate((zl, 1 - zl)):
        rows = []
        for block in range(4):
            first = 8 * which + 2 * block
            for core in range(2):
                halves = [
                    wide_ref[pl.ds(512 * core + first + half, 32, stride=16), :]
                    for half in range(2)
                ]
                rows.append(jnp.concatenate(halves, axis=1))
        table = jnp.concatenate(rows, axis=0)
        lhs_ref[:, 256 * side : 256 * side + 256] = table.T.astype(BF16)

    copies = []
    for chunk in range(4):
        cells = slice(BOUNDS[chunk], BOUNDS[chunk + 1])
        total = jnp.dot(lhs_ref[:, :256], own_ref[:, cells], preferred_element_type=F32)
        total = total + jnp.dot(lhs_ref[:, 256:], other_ref[:, cells], preferred_element_type=F32)
        done_ref[:, cells] = (total * scale).astype(BF16)
        copy = pltpu.make_async_copy(done_ref.at[:, cells], out_ref.at[:, cells], sems.at[chunk])
        copy.start()
        copies.append(copy)
    for copy in copies:
        copy.wait()


def rebuild(where, pred, own, other, scale):
    def body(*refs):
        rebuild_kernel(scale, *refs)

    return pl.pallas_call(
        body,
        out_shape=jax.ShapeDtypeStruct((256, CELLS), BF16),
        in_specs=[SMEM] + [VMEM] * 3,
        out_specs=pl.BlockSpec(memory_space=pl.ANY),
        scratch_shapes=[
            pltpu.VMEM((1024, 128), F32),
            pltpu.VMEM((256, 512), BF16),
            pltpu.VMEM((256, CELLS), BF16),
            pltpu.SemaphoreType.DMA((4,)),
        ],
        compiler_params=params(16),
        cost_estimate=pl.CostEstimate(flops=1 << 29, bytes_accessed=3 << 20, transcendentals=0),
    )(where, pred, own, other)


def on_device(fields_runs, eof_basis, weights_inv, design, new_settings, lscale, variance):
    zh, core = lax.axis_index("zh"), lax.axis_index("core")
    column = 32 * core + 8 * zh + lax.axis_index("y")
    where = jnp.stack([lax.axis_index("x"), column, lax.axis_index("zl"), zh, core])
    swap = [(0, 1), (1, 0)]

    fields_other = lax.ppermute(fields_runs, "zl", swap)
    basis = lax.all_to_all(
        pack(eof_basis.T, lscale, variance.reshape(1, 64)), "x", 0, 0, tiled=True
    ).reshape(256, WIDE)
    block = lax.ppermute(
        weights_inv.T.astype(BF16),
        ("zh", "x"),
        [(a * 4 + b, b * 4 + a) for a in range(4) for b in range(4)],
    )

    mine, theirs = project(where, fields_runs, fields_other, basis, 1.0 / math.sqrt(131072))
    theirs = lax.all_gather(theirs, "core", axis=0)
    parts = lax.all_to_all(slots(where, mine, theirs, block), ("zh", "y"), 0, 0, tiled=True)

    runs_feat, new_feat, aux = prepare(where, basis, design, new_settings)
    basis_other = lax.ppermute(basis, "zl", swap)

    pieces = lax.all_to_all(weights(parts, aux), ("x", "core"), 0, 0, tiled=True)
    pred = predict(runs_feat, new_feat, pieces, aux)
    pred = lax.all_to_all(pred.reshape(64, 8, 128), ("zh", "y", "zl"), 0, 0, tiled=True)
    pred = lax.all_gather(pred, "core", axis=0, tiled=True)
    return rebuild(
        where, pred.reshape(64, 2, 8, 128), basis, basis_other, 1.0 / math.sqrt(512)
    )


def solution(mesh):
    fine = Mesh(mesh.devices.reshape(4, 8, 2, 4, 2), GRID + COMP)
    placed = (
        P(COMP, GRID),
        P(GRID, COMP),
        P(None, GRID),
        P(),
        P(),
        P(None, COMP),
        P(COMP),
    )
    return jax.shard_map(
        on_device, mesh=fine, in_specs=placed, out_specs=P(COMP, GRID), check_vma=False
    )
```

```python
import math

import jax
import jax.numpy as jnp
from jax import lax
from jax.experimental import pallas as pl
from jax.experimental.pallas import tpu as pltpu
from jax.sharding import Mesh, PartitionSpec as P

GRID = ("zh", "y", "core")
COMP = ("x", "zl")
LOG2E = 1.4426950408889634
LN2 = 0.6931471805599453
F32 = jnp.float32
BF16 = jnp.bfloat16
HIGHEST = lax.Precision.HIGHEST
VMEM = pl.BlockSpec(memory_space=pltpu.VMEM)
SMEM = pl.BlockSpec(memory_space=pltpu.SMEM)
CELLS = 2048
WIDE = CELLS + 128
BOUNDS = (0, 512, 1024, 1536, 2048)


def params(mib):
    return pltpu.CompilerParams(vmem_limit_bytes=mib << 20)


def split3(value):
    first = value.astype(BF16)
    rest = value - first.astype(F32)
    second = rest.astype(BF16)
    third = (rest - second.astype(F32)).astype(BF16)
    return first, second, third


def pack_kernel(basis_ref, lscale_ref, variance_ref, out_ref):
    row = lax.broadcasted_iota(jnp.int32, (8, 64), 0)
    tail = jnp.where(row == 0, jnp.broadcast_to(variance_ref[...], (8, 64)), 0.0)
    value = jnp.concatenate([lscale_ref[...], tail], axis=0)
    pieces = jnp.concatenate([part.astype(F32) for part in split3(value)], axis=0)
    pieces = jnp.concatenate([pieces, jnp.zeros((80, 64), F32)], axis=0)
    side = jnp.concatenate([pieces, jnp.zeros((128, 64), F32)], axis=1).T[:64].astype(BF16)
    basis = basis_ref[...]
    for peer in range(4):
        out_ref[peer, :, :CELLS] = basis
        out_ref[peer, :, CELLS:] = side


def pack(basis, lscale, variance):
    return pl.pallas_call(
        pack_kernel,
        out_shape=jax.ShapeDtypeStruct((4, 64, WIDE), BF16),
        in_specs=[VMEM] * 3,
        out_specs=VMEM,
        compiler_params=params(60),
        cost_estimate=pl.CostEstimate(flops=0, bytes_accessed=5 << 18, transcendentals=0),
    )(basis, lscale, variance)


def project_kernel(scale, where_ref, own_ref, other_ref, basis_ref, mine_ref, theirs_ref, runs_ref):
    zl = where_ref[2]
    core = where_ref[4]
    for half, fields_ref in ((zl, own_ref), (1 - zl, other_ref)):
        for y in range(4):
            for side in range(2):
                first = 128 * lax.rem(side + core, 2) + 64 * half + 16 * y
                from_row = 32 * y + 16 * side
                runs_ref[pl.ds(pl.multiple_of(first, 16), 16), :] = fields_ref[
                    from_row : from_row + 16
                ]
    part = lax.dot_general(
        basis_ref[:, :CELLS], runs_ref[...], (((1,), (1,)), ((), ())), preferred_element_type=F32
    )
    mine_ref[...] = part[:, :128] * scale
    theirs_ref[...] = part[:, 128:] * scale


def project(where, own, other, basis, scale):
    def body(*refs):
        project_kernel(scale, *refs)

    half = jax.ShapeDtypeStruct((256, 128), F32)
    return pl.pallas_call(
        body,
        out_shape=(half, half),
        in_specs=[SMEM] + [VMEM] * 3,
        out_specs=(VMEM, VMEM),
        scratch_shapes=[pltpu.VMEM((256, CELLS), BF16)],
        compiler_params=params(16),
        cost_estimate=pl.CostEstimate(flops=1 << 28, bytes_accessed=1 << 21, transcendentals=0),
    )(where, own, other, basis)


def slots_kernel(where_ref, mine_ref, theirs_ref, block_ref, out_ref, held_ref, wide_ref, sems):
    for side in range(2):
        lanes = pl.ds(pl.multiple_of(256 * where_ref[3] + 128 * side, 128), 128)
        piece = block_ref[:, lanes]
        for chip in range(32):
            held_ref[chip, 16 + 16 * side : 32 + 16 * side, :] = piece
    lower = pltpu.make_async_copy(held_ref.at[:, 16:, :], out_ref.at[:, 16:, :], sems.at[0])
    lower.start()
    part = mine_ref[...] + theirs_ref[1 - where_ref[4]]
    high = part.astype(BF16).astype(F32)
    low = part - high
    for block in range(4):
        for core in range(2):
            first = 64 * block + 32 * core
            row = 4 * core + block
            wide_ref[pl.ds(row, 32, stride=16), :] = high[first : first + 32]
            wide_ref[pl.ds(row + 8, 32, stride=16), :] = low[first : first + 32]
    held_ref[:, :16, :] = wide_ref[...].astype(BF16).reshape(32, 16, 128)
    upper = pltpu.make_async_copy(held_ref.at[:, :16, :], out_ref.at[:, :16, :], sems.at[1])
    upper.start()
    lower.wait()
    upper.wait()


def slots(where, mine, theirs, block):
    return pl.pallas_call(
        slots_kernel,
        out_shape=jax.ShapeDtypeStruct((32, 48, 128), BF16),
        in_specs=[SMEM] + [VMEM] * 3,
        out_specs=pl.BlockSpec(memory_space=pl.ANY),
        scratch_shapes=[
            pltpu.VMEM((32, 48, 128), BF16),
            pltpu.VMEM((512, 128), F32),
            pltpu.SemaphoreType.DMA((2,)),
        ],
        compiler_params=params(16),
        cost_estimate=pl.CostEstimate(flops=1 << 20, bytes_accessed=1 << 20, transcendentals=0),
    )(where, mine, theirs, block)


def weights_kernel(parts_ref, after_ref, out_ref, winv_ref):
    for chip in range(32):
        zh, y = chip // 8, chip % 8
        for side in range(2):
            winv_ref[16 * y : 16 * y + 16, 256 * zh + 128 * side : 256 * zh + 128 * side + 128] = (
                parts_ref[chip, 16 + 16 * side : 32 + 16 * side, :]
            )
    both = jnp.sum(parts_ref[:, :16, :].astype(F32), axis=0)
    coef = both[:8] + both[8:]
    rows = jnp.concatenate(
        [p.astype(F32) for p in split3(coef)] + [jnp.zeros((8, 128), F32)], axis=0
    ).astype(BF16)
    full = jnp.dot(rows, winv_ref[...], preferred_element_type=F32)
    full = (full[16:24] + full[8:16]) + full[:8]
    for core in range(2):
        for block in range(4):
            for tile in range(8):
                piece = full[4 * core + block : 4 * core + block + 1, 128 * tile : 128 * tile + 128]
                for peer in range(4):
                    row = 8 * block + tile
                    out_ref[4 * core + peer, row : row + 1, :] = piece


def weights(parts, after):
    return pl.pallas_call(
        weights_kernel,
        out_shape=jax.ShapeDtypeStruct((8, 32, 128), F32),
        in_specs=[VMEM, pl.BlockSpec(memory_space=pl.ANY)],
        out_specs=VMEM,
        scratch_shapes=[pltpu.VMEM((128, 1024), BF16)],
        compiler_params=params(16),
        cost_estimate=pl.CostEstimate(flops=1 << 23, bytes_accessed=1 << 20, transcendentals=0),
    )(parts, after)


def prepare_kernel(where_ref, side_ref, design_ref, new_ref, runs_ref, new_out_ref, aux_ref, wide_ref):
    wide_ref[...] = side_ref[...].astype(F32)
    runs = design_ref[...] - 0.5
    first, second, third = split3(jnp.concatenate([runs, runs * runs], axis=0))
    row = lax.broadcasted_iota(jnp.int32, (32, 1024), 0)
    ones = jnp.where(row < 3, 1.0, 0.0)
    parts = [first, first, first, second, second, third]
    table = jnp.concatenate([p.astype(F32) for p in parts] + [ones], axis=0)
    runs_ref[...] = table.T.astype(BF16)
    new = new_ref[:, pl.ds(pl.multiple_of(where_ref[0] * 512, 512), 512)] - 0.5
    aux_ref[...] = jnp.zeros((8, 128), F32)
    row = lax.broadcasted_iota(jnp.int32, (32, 512), 0)
    for block in range(4):
        mine = wide_ref[pl.ds(64 * block + where_ref[1], 1), :]
        column = jnp.broadcast_to(mine, (128, 128)).T
        value = (column[0:16] + column[16:32]) + column[32:48]
        aux_ref[block : block + 1, :] = value[8:9] * LN2
        lscale = value[:8]
        weight = (3.0 * LOG2E * LOG2E) / (lscale * lscale)
        weight = jnp.concatenate([weight] * 4, axis=1)
        scaled = weight * new
        first, second, third = split3(jnp.concatenate([-2.0 * scaled, weight], axis=0))
        square = jnp.broadcast_to(jnp.sum(scaled * new, axis=0, keepdims=True), (32, 512))
        lead, mid, low = [p.astype(F32) for p in split3(square)]
        tail = jnp.where(row == 0, lead, jnp.where(row == 1, mid, jnp.where(row == 2, low, 0.0)))
        new_out_ref[block] = jnp.concatenate(
            [first, second, third, first, second, first, tail.astype(BF16)], axis=0
        )


def prepare(where, basis, design, new_settings):
    return pl.pallas_call(
        prepare_kernel,
        grid=(1,),
        out_shape=(
            jax.ShapeDtypeStruct((1024, 128), BF16),
            jax.ShapeDtypeStruct((4, 128, 512), BF16),
            jax.ShapeDtypeStruct((8, 128), F32),
        ),
        in_specs=[
            SMEM,
            pl.BlockSpec((256, 128), lambda i: (0, CELLS // 128)),
            pl.BlockSpec((8, 1024), lambda i: (0, 0)),
            pl.BlockSpec((8, 2048), lambda i: (0, 0)),
        ],
        out_specs=(
            pl.BlockSpec((1024, 128), lambda i: (0, 0)),
            pl.BlockSpec((4, 128, 512), lambda i: (0, 0, 0)),
            pl.BlockSpec((8, 128), lambda i: (0, 0)),
        ),
        scratch_shapes=[pltpu.VMEM((256, 128), F32)],
        compiler_params=params(16),
        cost_estimate=pl.CostEstimate(flops=1 << 24, bytes_accessed=1 << 20, transcendentals=0),
    )(where, basis, design, new_settings)


def predict_kernel(runs_ref, new_ref, pieces_ref, aux_ref, out_ref, spread_ref, pred_ref):
    both = jnp.sum(pieces_ref[...], axis=0)
    parts = [p.astype(F32) for p in split3(both)]
    table = jnp.concatenate(parts + [jnp.zeros((32, 128), F32)], axis=0).T
    row = lax.broadcasted_iota(jnp.int32, (128, 512), 0)
    col = lax.broadcasted_iota(jnp.int32, (128, 512), 1)
    pick = ((row % 32 == 8 * (col // 128)) & (row < 96)).astype(BF16)
    for tile in range(8):
        rolled = pltpu.roll(table, (128 - tile) % 128, axis=1).astype(BF16)
        spread_ref[128 * tile : 128 * tile + 128, :] = jnp.dot(
            rolled, pick, preferred_element_type=F32
        )

    for block in range(4):
        acc = [jnp.zeros((8, 128), F32)] * 4
        for chunk in range(16):
            rows = slice(64 * chunk, 64 * chunk + 64)
            weight = spread_ref[rows, 128 * block : 128 * block + 128]
            sq = jnp.dot(runs_ref[rows], new_ref[block], preferred_element_type=F32)
            sq = jnp.maximum(sq, 1e-30)
            dist = sq * lax.rsqrt(sq)
            values = (LOG2E + dist) * jnp.exp2(-dist)
            for tile in range(4):
                prod = values[:, 128 * tile : 128 * tile + 128] * weight
                acc[tile] = acc[tile] + jnp.sum(prod.reshape(8, 8, 128), axis=0)
        for tile in range(4):
            where = (tile // 2) * 8 + 2 * block + tile % 2
            total = jnp.sum(acc[tile], axis=0, keepdims=True)
            pred_ref[where : where + 1, :] = total * aux_ref[block : block + 1, :]

    tile = pred_ref[...].astype(BF16).reshape(1, 2, 8, 128)
    out_ref[...] = jnp.broadcast_to(tile, (32, 2, 8, 128))


def predict(runs_feat, new_feat, pieces, aux):
    return pl.pallas_call(
        predict_kernel,
        out_shape=jax.ShapeDtypeStruct((32, 2, 8, 128), BF16),
        in_specs=[VMEM] * 4,
        out_specs=VMEM,
        scratch_shapes=[pltpu.VMEM((1024, 512), F32), pltpu.VMEM((16, 128), F32)],
        compiler_params=params(16),
        cost_estimate=pl.CostEstimate(
            flops=1 << 28, bytes_accessed=1 << 20, transcendentals=1 << 22
        ),
    )(runs_feat, new_feat, pieces, aux)


def rebuild_kernel(
    scale, where_ref, pred_ref, own_ref, other_ref, out_ref, wide_ref, lhs_ref, done_ref, sems
):
    wide_ref[...] = pred_ref[...].astype(F32).reshape(1024, 128)
    zl = where_ref[2]
    for side, which in enumerate((zl, 1 - zl)):
        rows = []
        for block in range(4):
            first = 8 * which + 2 * block
            for core in range(2):
                halves = [
                    wide_ref[pl.ds(512 * core + first + half, 32, stride=16), :]
                    for half in range(2)
                ]
                rows.append(jnp.concatenate(halves, axis=1))
        table = jnp.concatenate(rows, axis=0)
        lhs_ref[:, 256 * side : 256 * side + 256] = table.T.astype(BF16)

    copies = []
    for chunk in range(4):
        cells = slice(BOUNDS[chunk], BOUNDS[chunk + 1])
        total = jnp.dot(lhs_ref[:, :256], own_ref[:, cells], preferred_element_type=F32)
        total = total + jnp.dot(lhs_ref[:, 256:], other_ref[:, cells], preferred_element_type=F32)
        done_ref[:, cells] = (total * scale).astype(BF16)
        copy = pltpu.make_async_copy(done_ref.at[:, cells], out_ref.at[:, cells], sems.at[chunk])
        copy.start()
        copies.append(copy)
    for copy in copies:
        copy.wait()


def rebuild(where, pred, own, other, scale):
    def body(*refs):
        rebuild_kernel(scale, *refs)

    return pl.pallas_call(
        body,
        out_shape=jax.ShapeDtypeStruct((256, CELLS), BF16),
        in_specs=[SMEM] + [VMEM] * 3,
        out_specs=pl.BlockSpec(memory_space=pl.ANY),
        scratch_shapes=[
            pltpu.VMEM((1024, 128), F32),
            pltpu.VMEM((256, 512), BF16),
            pltpu.VMEM((256, CELLS), BF16),
            pltpu.SemaphoreType.DMA((4,)),
        ],
        compiler_params=params(16),
        cost_estimate=pl.CostEstimate(flops=1 << 29, bytes_accessed=3 << 20, transcendentals=0),
    )(where, pred, own, other)


def on_device(fields_runs, eof_basis, weights_inv, design, new_settings, lscale, variance):
    zh, core = lax.axis_index("zh"), lax.axis_index("core")
    column = 32 * core + 8 * zh + lax.axis_index("y")
    where = jnp.stack([lax.axis_index("x"), column, lax.axis_index("zl"), zh, core])
    swap = [(0, 1), (1, 0)]

    fields_other = lax.ppermute(fields_runs, "zl", swap)
    basis = lax.all_to_all(
        pack(eof_basis.T, lscale, variance.reshape(1, 64)), "x", 0, 0, tiled=True
    ).reshape(256, WIDE)
    block = lax.ppermute(
        weights_inv.T.astype(BF16),
        ("zh", "x"),
        [(a * 4 + b, b * 4 + a) for a in range(4) for b in range(4)],
    )

    mine, theirs = project(where, fields_runs, fields_other, basis, 1.0 / math.sqrt(131072))
    theirs = lax.all_gather(theirs, "core", axis=0)
    parts = lax.all_to_all(slots(where, mine, theirs, block), ("zh", "y"), 0, 0, tiled=True)

    runs_feat, new_feat, aux = prepare(where, basis, design, new_settings)
    basis_other = lax.ppermute(basis, "zl", swap)

    pieces = lax.all_to_all(weights(parts, aux), ("core", "x"), 0, 0, tiled=True)
    pred = predict(runs_feat, new_feat, pieces, aux)
    pred = lax.all_to_all(pred.reshape(64, 8, 128), ("zh", "y", "zl"), 0, 0, tiled=True)
    pred = lax.all_gather(pred, "core", axis=0, tiled=True)
    return rebuild(
        where, pred.reshape(64, 2, 8, 128), basis, basis_other, 1.0 / math.sqrt(512)
    )


def solution(mesh):
    fine = Mesh(mesh.devices.reshape(4, 8, 2, 4, 2), GRID + COMP)
    placed = (
        P(COMP, GRID),
        P(GRID, COMP),
        P(None, GRID),
        P(),
        P(),
        P(None, COMP),
        P(COMP),
    )
    return jax.shard_map(
        on_device, mesh=fine, in_specs=placed, out_specs=P(COMP, GRID), check_vma=False
    )
```
